32 devices in a mesh: seq: 8 (over z, y), tp: 4 (over x, core).
Axes of the slice: x: 2, y: 2, z: 4, core: 2. Of those that a mesh axis runs over, the one named last changes fastest.
Arguments:
- tokens: bfloat16 [1024, 1024], P('seq'), may hold values from -6 to 6
- norm_gain: float32 [1024], replicated, may hold values from 0.25 to 1.75
- w_qkv: bfloat16 [1024, 3, 1024], P(None, None, 'tp'), may hold values from -1 to 1
- w_out: bfloat16 [1024, 1024], P('tp'), may hold values from -0.1875 to 0.1875
- head_bias: float32 [2, 16], P(None, 'tp'), may hold values from -1.5 to 1.5
- kv_pool: bfloat16 [32, 128, 2, 1024], P('seq', None, None, 'tp'), may hold values from -6 to 6
- key_variate: int32 [32, 128], P('seq'), may hold values from 0 to 7
- page_table: int32 [8, 4], P('seq'), may hold values from 0 to 3, each once within a row
- node_len: int32 [8], P('seq'), may hold values from 1 to 512, 3072 in all
- path_nodes: int32 [1024, 3], P('seq'), may hold values from 0 to 7, all different within a row; in each aligned block of 128 rows (0 to 127, 128 to 255, ...) at most 128 rows name the same one
- query_variate: int32 [1024], P('seq'), may hold values from 0 to 7
Outputs:
- updated: bfloat16 [1024, 1024], P('seq')
The draws below stay inside these ranges and needn't reach their ends.
Inputs may be any that keep to these rules, and one draw needn't show every extreme that they name: `path_nodes`: each row names three different nodes; the rows of one device name one node at most 128 times, a bound that some block reaches. `page_table`: each row is a permutation. `node_len`: some node holds exactly 512 tokens.
All inputs are finite; a program needn't handle non-finite values. No bound on the sum of `node_len` on one device may be relied on, other than what follows from the above.
Results may differ from the reference program's by a relative error of at most 0.0033.
The reference program's roundings to bfloat16 on the way count: a program that leaves them out, or rounds other values in their place, can miss the bound.
Values may be sent and summed in bfloat16 or wider, within the bound.
No kernel may reach another device: no remote copies, remote signals or barrier semaphores. Data moves between devices by JAX's collectives and lax.ppermute only.
A program may use at most 64 MiB of HBM per device.

```python
import math
import jax
import jax.numpy as jnp
import numpy as np
from jax import lax

D = 1024
H = 16
HD = 64
TOK_DEV = 128
PAGE = 128
PAGES_NODE = 4
VARIATES = 8
NODE_LEN = 512
CAP = 128
TOKENS = 1024
N_SEQ = 8


def draw_w_qkv(key, part):
    first = jax.random.fold_in(key, 11)
    base = jnp.clip(jax.random.normal(first, (D, 3, H * HD), jnp.float32), -4.0, 4.0) * D ** (-0.5)
    return base.astype(jnp.bfloat16)


def draw_kv_pool(key, part):
    rows = N_SEQ * PAGES_NODE
    first = jax.random.fold_in(key, 21)
    third = jax.random.fold_in(key, 23)
    values = jnp.clip(jax.random.normal(third, (rows, PAGE, H * HD), jnp.float32), -6.0, 6.0)
    keys = jnp.clip(jax.random.normal(first, (rows, PAGE, H * HD), jnp.float32), -6.0, 6.0)
    return jnp.stack([keys, values], axis=2).astype(jnp.bfloat16)


def place_ends(result, stream_key, low, high):
    dims = result.shape
    index_at = [jax.random.randint(jax.random.fold_in(stream_key, axis), (), 0, dims[axis]) for axis in range(len(dims))]
    result = result.at[tuple(index_at)].set(low)
    longest = dims.index(max(dims))
    index_at[longest] = (index_at[longest] + 1) % dims[longest]
    return result.at[tuple(index_at)].set(high)


def level_of(stream_key, shape, pieces, least, high):
    level, own = 1.0, jax.random.fold_in(stream_key, 6)
    for position, blocks in pieces:
        steps = jnp.exp(jax.random.uniform(jax.random.fold_in(own, position), (blocks,), jnp.float32, least / len(pieces), high / len(pieces)))
        level = level * jnp.repeat(steps, shape[position] // blocks).reshape([-1 if axis == position else 1 for axis in range(len(shape))])
    return level


def length_profile(count, total, most, skew):
    loads = [(1 << 20) // math.isqrt(grade ** skew) + 1 for grade in range(2, count + 1)]
    rest, given = total - most - (count - 1), [1] * (count - 1)
    while rest > 0:
        candidates = [i for i in range(count - 1) if given[i] < most]
        whole, left = sum([loads[i] for i in candidates]), rest
        for i in candidates:
            addition = min(most - given[i], max(1, left * loads[i] // whole), rest)
            given[i] = given[i] + addition
            rest = rest - addition
    return np.array([most] + given)


def uneven(rng, number_of, total, bound, skew):
    if number_of == 2:
        one = jax.random.randint(rng, (), max(1, total - bound), min(bound, total - 1) + 1)
        return jnp.stack([one, total - one])
    lengths = jnp.asarray(length_profile(number_of, total, bound, skew), jnp.int32)
    twos = (number_of - 1) // 2
    donor, sink = lengths[1:1 + 2 * twos:2], lengths[2:2 + 2 * twos:2]
    room = jnp.minimum(donor - 1, bound - sink)
    shifted = jax.random.randint(jax.random.fold_in(rng, 1), (twos,), 0, 1 << 20) % (room + 1)
    lengths = lengths.at[1:1 + 2 * twos:2].set(donor - shifted).at[2:2 + 2 * twos:2].set(sink + shifted)
    return lengths[jax.random.permutation(jax.random.fold_in(rng, 2), number_of)]


def assign_block(own_key, own, number, rows, number_of, top, bound, slope):
    sequence = jax.random.permutation(own_key, number_of)
    heavy_load, usual = load_shares(number_of, rows * top, bound, slope, True), load_shares(number_of, rows * top, bound, slope, False)
    places = jnp.arange(number_of)

    def named(tallies, turn):
        used = int((tallies > 0).sum())
        fixed = max(1, used // 4)
        moved = fixed + (places - fixed + turn * (used - fixed)) % max(1, number_of - fixed)
        return jnp.zeros((number_of,), jnp.int32).at[sequence[jnp.where(places < fixed, places, moved)]].set(jnp.asarray(tallies, jnp.int32))

    tallies = jnp.where(number % 4 == 0, named(heavy_load, number // 4), named(usual, number - number // 4 - 1))
    mixed = jax.random.permutation(jax.random.fold_in(own, 3), number_of)
    donor, taker = mixed[0:number_of // 2 * 2:2], mixed[1:number_of // 2 * 2:2]
    slack = jnp.minimum(tallies[donor] - 1, bound - tallies[taker]) // 2
    slack = jnp.where((donor == sequence[0]) | (taker == sequence[0]) | (tallies[taker] == 0), 0, jnp.maximum(slack, 0))
    moved = jax.random.randint(jax.random.fold_in(own, 4), (number_of // 2,), 0, 1 << 20) % (slack + 1)
    tallies = tallies.at[donor].add(-moved).at[taker].add(moved)
    members = jnp.searchsorted(jnp.cumsum(tallies), jnp.arange(rows * top), side="right").astype(jnp.int32)
    grid = members.reshape(top, rows).T
    grid = grid[jax.random.permutation(jax.random.fold_in(own, 1), rows)]
    turn = jax.random.randint(jax.random.fold_in(own, 2), (rows, 1), 0, top)
    return jnp.take_along_axis(grid, (jnp.arange(top)[None, :] + turn) % top, axis=1)


def load_shares(amount, total, reach, slope, full):
    portions = [(1 << 20) // math.isqrt(grade ** slope) + 1 for grade in range(1, amount + 1)]
    largest = reach if full else min(reach, max(-(-total // amount), total * portions[0] // sum(portions)))
    least = 1 if total - largest >= amount - 1 else 0
    counts, surplus = [largest] + [least] * (amount - 1), total - largest - least * (amount - 1)
    while surplus > 0:
        free = [i for i in range(1, amount) if counts[i] < largest] or [i for i in range(1, amount) if counts[i] < reach]
        mass, budget = sum([portions[i] for i in free]), surplus
        for i in free:
            more = min(reach - counts[i], max(1, budget * portions[i] // mass), surplus)
            counts[i] = counts[i] + more
            surplus = surplus - more
    return np.array(counts)


def normal_values(key, shape, deviation, limit, split=(), held_as=jnp.bfloat16):
    loudness = level_of(key, shape, split, -0.22, 0.18) if split else 1.0
    result = jax.random.normal(key, shape, jnp.float32) * deviation * loudness
    return jnp.minimum(jnp.maximum(result, -limit), limit).astype(held_as)


def setup_inputs(seed: int = 0) -> dict:
    arg_keys = jax.random.split(jax.random.key(seed), 12)
    tokens = normal_values(arg_keys[0], (TOKENS, D), 1.0, 6.0, ((0, 8),))
    norm_gain = jnp.clip(1.0 + 0.15 * jax.random.normal(arg_keys[1], (D,), jnp.float32), 0.25, 1.75)
    w_qkv = draw_w_qkv(jax.random.fold_in(arg_keys[11], 71), 0)
    w_out = normal_values(arg_keys[3], (H * HD, D), (H * HD) ** -0.5, 0.1875, ((0, 4),))
    head_bias = jnp.clip(jax.random.uniform(arg_keys[4], (2, H), jnp.float32, -1.5, 1.5) * level_of(arg_keys[4], (2, H), ((1, 4),), -0.4, 0.0), -1.5, 1.5)
    kv_pool = draw_kv_pool(jax.random.fold_in(arg_keys[11], 71), 0)
    key_variate = place_ends(jax.random.randint(arg_keys[6], (N_SEQ * PAGES_NODE, PAGE), 0, VARIATES), jax.random.fold_in(arg_keys[6], 1), 0, VARIATES - 1).astype(jnp.int32)
    page_table = jax.vmap(lambda own: jax.random.permutation(own, PAGES_NODE))(jax.random.split(arg_keys[7], N_SEQ)).reshape((N_SEQ, PAGES_NODE)).astype(jnp.int32)
    node_len = uneven(arg_keys[8], N_SEQ, N_SEQ * NODE_LEN * 3 // 4, NODE_LEN, 2).astype(jnp.int32)
    path_nodes_keys = jax.random.split(jax.random.fold_in(arg_keys[9], 1), TOKENS // TOK_DEV)
    path_nodes_turns = jax.random.permutation(jax.random.fold_in(arg_keys[9], 3), TOKENS // TOK_DEV)
    path_nodes = jax.vmap(lambda own, number: assign_block(jax.random.fold_in(arg_keys[9], 2), own, number, TOK_DEV, N_SEQ, 3, CAP, 2))(path_nodes_keys, path_nodes_turns).reshape((TOKENS, 3))
    query_variate = place_ends(jax.random.randint(arg_keys[10], (TOKENS,), 0, VARIATES), jax.random.fold_in(arg_keys[10], 1), 0, VARIATES - 1).astype(jnp.int32)
    return {"tokens": tokens, "norm_gain": norm_gain, "w_qkv": w_qkv, "w_out": w_out, "head_bias": head_bias, "kv_pool": kv_pool, "key_variate": key_variate, "page_table": page_table, "node_len": node_len, "path_nodes": path_nodes, "query_variate": query_variate}


def head_attend(qh, kh, vh, same, bias_same, bias_diff, valid):
    scores = jnp.dot(qh, kh.T, preferred_element_type=jnp.float32) * HD ** (-0.5)
    scores = scores + jnp.where(same, bias_same, bias_diff)
    scores = jnp.where(valid[None, :], scores, -1e+30)
    peak = lax.optimization_barrier(jnp.max(scores, axis=1))
    weights = jnp.exp(scores - peak[:, None])
    total = lax.optimization_barrier(jnp.sum(weights, axis=1))
    mixed = jnp.dot(weights.astype(jnp.bfloat16), vh, preferred_element_type=jnp.float32) / total[:, None]
    mixed = lax.optimization_barrier(mixed.astype(jnp.bfloat16))
    return (mixed, peak, total)

def reference(tokens, norm_gain, w_qkv, w_out, head_bias, kv_pool, key_variate, page_table, node_len, path_nodes, query_variate):
    xf = tokens.astype(jnp.float32)
    normed = (xf * lax.rsqrt(lax.optimization_barrier(jnp.mean(xf * xf, axis=1, keepdims=True)) + 1e-05) * norm_gain).astype(jnp.bfloat16)
    qkv = jnp.dot(normed, w_qkv.reshape(D, 3 * H * HD), preferred_element_type=jnp.float32).astype(jnp.bfloat16)
    qkv = qkv.reshape(TOKENS, 3, H, HD)
    query, key, value = (qkv[:, 0], qkv[:, 1], qkv[:, 2])
    pool = kv_pool.reshape(N_SEQ, PAGES_NODE, PAGE, 2, H, HD)
    pool_var = key_variate.reshape(N_SEQ, PAGES_NODE, PAGE)
    flat = path_nodes.reshape(-1)
    items = 3 * TOKENS
    recv = N_SEQ * CAP
    heads_q = jnp.moveaxis(query, 1, 0)

    def one_node(n, carry):
        outs, peaks, totals = carry
        order = lax.dynamic_index_in_dim(page_table, n, 0, keepdims=False)
        pages = lax.dynamic_index_in_dim(pool, n, 0, keepdims=False)[order].reshape(NODE_LEN, 2, H, HD)
        kvar = lax.dynamic_index_in_dim(pool_var, n, 0, keepdims=False)[order].reshape(NODE_LEN)
        length = lax.dynamic_index_in_dim(node_len, n, 0, keepdims=False)
        valid = jnp.arange(NODE_LEN, dtype=jnp.int32) < length
        hits = flat == n
        count = jnp.sum(hits.astype(jnp.int32))
        where_at = jnp.nonzero(hits, size=recv, fill_value=0)[0].astype(jnp.int32)
        rows = where_at // 3
        qvar = query_variate[rows]
        same = qvar[:, None] == kvar[None, :]
        qn = heads_q[:, rows]
        kn = jnp.moveaxis(pages[:, 0], 1, 0)
        vn = jnp.moveaxis(pages[:, 1], 1, 0)

        def per_head(xs):
            return head_attend(xs[0], xs[1], xs[2], same, xs[3], xs[4], valid)
        mixed, peak, total = lax.map(per_head, (qn, kn, vn, head_bias[1], head_bias[0]))
        ok = jnp.arange(recv, dtype=jnp.int32) < count
        target = jnp.where(ok, where_at, items).astype(jnp.int32)
        outs = outs.at[target].set(jnp.moveaxis(mixed, 0, 1).astype(jnp.float32), mode='drop')
        peaks = peaks.at[target].set(peak.T, mode='drop')
        totals = totals.at[target].set(total.T, mode='drop')
        return (outs, peaks, totals)
    start = (jnp.zeros((items, H, HD), jnp.float32), jnp.zeros((items, H), jnp.float32), jnp.ones((items, H), jnp.float32))
    outs, peaks, totals = lax.fori_loop(0, N_SEQ, one_node, start)
    own_peak = lax.optimization_barrier(jnp.sum(query.astype(jnp.float32) * key.astype(jnp.float32), axis=2)) * HD ** (-0.5) + head_bias[1][None, :]
    all_o = jnp.concatenate([value.astype(jnp.float32)[:, None], outs.reshape(TOKENS, 3, H, HD)], axis=1)
    all_m = jnp.concatenate([own_peak[:, None], peaks.reshape(TOKENS, 3, H)], axis=1)
    all_l = jnp.concatenate([jnp.ones((TOKENS, 1, H), jnp.float32), totals.reshape(TOKENS, 3, H)], axis=1)
    top = lax.optimization_barrier(jnp.max(all_m, axis=1, keepdims=True))
    scale = all_l * jnp.exp(all_m - top)
    attn = (lax.optimization_barrier(jnp.sum(scale[..., None] * all_o, axis=1)) / lax.optimization_barrier(jnp.sum(scale, axis=1))[..., None]).astype(jnp.bfloat16)
    projected = jnp.dot(attn.reshape(TOKENS, H * HD), w_out, preferred_element_type=jnp.float32)
    return (xf + projected).astype(jnp.bfloat16)
```

```python
import jax
import jax.numpy as jnp
from jax import lax
from jax.experimental import pallas as pl
from jax.experimental.pallas import tpu as pltpu
from jax.sharding import PartitionSpec as P

HD = 64


def head_attend(qh, kh, vh, same, bias_same, bias_diff, valid):
    scores = jnp.dot(qh, kh.T, preferred_element_type=jnp.float32) * HD ** (-0.5)
    scores = scores + jnp.where(same, bias_same, bias_diff)
    scores = jnp.where(valid[None, :], scores, -1e30)
    peak = jnp.max(scores, axis=1)
    weights = jnp.exp(scores - peak[:, None])
    total = jnp.sum(weights, axis=1)
    mixed = (
        jnp.dot(weights.astype(jnp.bfloat16), vh, preferred_element_type=jnp.float32)
        / total[:, None]
    )
    mixed = lax.optimization_barrier(mixed.astype(jnp.bfloat16))
    return (mixed, peak, total)


def place_rows(dest, values, variates, owners, slots):
    onehot = (dest[:, None] == jnp.arange(owners, dtype=jnp.int32)[None, :]).astype(jnp.int32)
    before = jnp.cumsum(onehot, axis=0) - onehot
    slot = jnp.sum(before * onehot, axis=1)
    flat = dest * slots + slot
    width = values.shape[1]
    qbuf = (
        jnp.zeros((owners * slots, width), jnp.bfloat16)
        .at[flat]
        .set(values)
        .reshape(owners, slots, width)
    )
    vbuf = jnp.zeros((owners * slots,), jnp.int32).at[flat].set(variates).reshape(owners, slots)
    return (qbuf, vbuf, flat)


def routed_body(
    tokens,
    norm_gain,
    w_qkv,
    w_out,
    head_bias,
    kv_pool,
    key_variate,
    page_table,
    node_len,
    path_nodes,
    query_variate,
):
    tok_rows, width = tokens.shape
    heads_here = w_qkv.shape[2] // HD
    owners = lax.axis_size("seq")
    slots = min(tok_rows, 8 * tok_rows // owners)
    xf = tokens.astype(jnp.float32)
    normed = (xf * lax.rsqrt(jnp.mean(xf * xf, axis=1, keepdims=True) + 1e-05) * norm_gain).astype(
        jnp.bfloat16
    )
    qkv = jnp.dot(
        normed, w_qkv.reshape(width, 3 * heads_here * HD), preferred_element_type=jnp.float32
    ).astype(jnp.bfloat16)
    qkv = qkv.reshape(tok_rows, 3, heads_here, HD)
    query, key, value = (qkv[:, 0], qkv[:, 1], qkv[:, 2])
    order = page_table[0]
    node_slots = kv_pool.shape[0] * kv_pool.shape[1]
    pages = kv_pool[order].reshape(node_slots, 2, heads_here, HD)
    node_keys = jnp.moveaxis(pages[:, 0], 1, 0)
    node_values = jnp.moveaxis(pages[:, 1], 1, 0)
    key_var = key_variate[order].reshape(node_slots)
    valid = jnp.arange(node_slots, dtype=jnp.int32) < node_len[0]
    qflat = query.reshape(tok_rows, heads_here * HD)
    out_list, peak_list, total_list = ([], [], [])
    for level in range(3):
        qbuf, vbuf, flat = place_rows(path_nodes[:, level], qflat, query_variate, owners, slots)
        owner_qbuf = lax.all_to_all(qbuf, "seq", split_axis=0, concat_axis=0, tiled=True)
        owner_vbuf = lax.all_to_all(vbuf, "seq", split_axis=0, concat_axis=0, tiled=True)
        sources, count, cols = owner_qbuf.shape
        rows = sources * count
        heads_q = jnp.moveaxis(owner_qbuf.reshape(rows, heads_here, HD), 1, 0)
        same = owner_vbuf.reshape(rows)[:, None] == key_var[None, :]

        def per_head(xs):
            return head_attend(xs[0], xs[1], xs[2], same, xs[3], xs[4], valid)

        mixed, peak, total = lax.map(
            per_head, (heads_q, node_keys, node_values, head_bias[1], head_bias[0])
        )
        mixed = jnp.moveaxis(mixed, 0, 1).reshape(sources, count, cols)
        peak = peak.T.reshape(sources, count, heads_here)
        total = total.T.reshape(sources, count, heads_here)
        mixed_back = lax.all_to_all(mixed, "seq", split_axis=0, concat_axis=0, tiled=True)
        peak_back = lax.all_to_all(peak, "seq", split_axis=0, concat_axis=0, tiled=True)
        total_back = lax.all_to_all(total, "seq", split_axis=0, concat_axis=0, tiled=True)
        mixed = mixed_back
        peak = peak_back
        total = total_back
        out_list.append(mixed.reshape(owners * slots, -1)[flat].reshape(tok_rows, heads_here, HD))
        peak_list.append(peak.reshape(owners * slots, heads_here)[flat])
        total_list.append(total.reshape(owners * slots, heads_here)[flat])
    outs = jnp.stack(out_list, axis=1)
    peaks = jnp.stack(peak_list, axis=1)
    totals = jnp.stack(total_list, axis=1)
    own_peak = (
        jnp.sum(query.astype(jnp.float32) * key.astype(jnp.float32), axis=2) * HD ** (-0.5)
        + head_bias[1][None, :]
    )
    all_o = jnp.concatenate([value.astype(jnp.float32)[:, None], outs.astype(jnp.float32)], axis=1)
    all_m = jnp.concatenate([own_peak[:, None], peaks], axis=1)
    all_l = jnp.concatenate([jnp.ones((tok_rows, 1, heads_here), jnp.float32), totals], axis=1)
    top = jnp.max(all_m, axis=1, keepdims=True)
    scale = all_l * jnp.exp(all_m - top)
    attn = (jnp.sum(scale[..., None] * all_o, axis=1) / jnp.sum(scale, axis=1)[..., None]).astype(
        jnp.bfloat16
    )
    partial_sum = jnp.dot(
        attn.reshape(tok_rows, heads_here * HD), w_out, preferred_element_type=jnp.float32
    )
    total_sum = lax.psum(partial_sum, "tp")
    return (xf + total_sum).astype(jnp.bfloat16)


BF16, F32, I32 = jnp.bfloat16, jnp.float32, jnp.int32
AUX = 16
FAR = -1e30
VMEM = pl.BlockSpec(memory_space=pltpu.VMEM)


def call(kernel, outs, *args, flops=1 << 20, scratch=()):
    single = not isinstance(outs, (tuple, list))
    moved = sum(a.size * a.dtype.itemsize for a in args)
    return pl.pallas_call(
        kernel,
        out_shape=outs,
        in_specs=[VMEM] * len(args),
        out_specs=VMEM if single else [VMEM] * len(outs),
        scratch_shapes=list(scratch),
        compiler_params=pltpu.CompilerParams(vmem_limit_bytes=32 << 20),
        cost_estimate=pl.CostEstimate(flops=flops, bytes_accessed=moved, transcendentals=0),
    )(*args)


def shape(*dims, dtype=BF16):
    return jax.ShapeDtypeStruct(dims, dtype)


def normalise(tok_ref, gain_ref):
    x = tok_ref[...].astype(F32)
    r = lax.rsqrt(jnp.mean(x * x, axis=1, keepdims=True) + 1e-05)
    return (x * r * gain_ref[...]).astype(BF16)


def query_kernel(tok_ref, gain_ref, w_ref, aux_ref, msg_ref, normed_ref):
    normed = normalise(tok_ref, gain_ref)
    normed_ref[...] = normed
    q = jnp.dot(normed, w_ref[...], preferred_element_type=F32).astype(BF16)
    cols = q.shape[1]
    msg_ref[:cols, :] = (q.astype(F32) * HD ** (-0.5)).T.astype(BF16)
    msg_ref[cols:, :] = aux_ref[...]


def own_kernel(normed_ref, wk_ref, wv_ref, k_ref, v_ref):
    normed = normed_ref[...]
    for w_ref, out_ref in ((wk_ref, k_ref), (wv_ref, v_ref)):
        out_ref[...] = jnp.dot(normed, w_ref[...], preferred_element_type=F32).astype(BF16).astype(F32).T.astype(BF16)


def split3(x):
    a = x.astype(BF16)
    r = x - a.astype(F32)
    b = r.astype(BF16)
    c = (r - b.astype(F32)).astype(BF16)
    return a, b, c


def slot_terms(code_ref):
    pages, page = code_ref.shape
    blocks = []
    lane = lax.broadcasted_iota(I32, (page, 128), 1)
    for p in range(pages):
        row = code_ref[p : p + 1, :]
        sub = lax.broadcasted_iota(I32, (128, page), 0)
        code = jnp.broadcast_to(row, (128, page))
        hit = (code == sub % 8) & (sub < 24)
        term = jnp.where(hit | ((sub >= 24) & (sub < 27)), 1.0, 0.0)
        term = jnp.where((sub == 27) & (code == 8), FAR, term)
        blocks.append(term.T.astype(BF16))
    return jnp.concatenate(blocks, axis=0)


def row_terms(bias_ref, head, variate):
    same, other = bias_ref[1, head], bias_ref[0, head]
    rows = variate.shape[1]
    sub = lax.broadcasted_iota(I32, (128, rows), 0)
    hit = (variate == sub % 8) & (sub < 24)
    one = jnp.zeros((128, rows), F32)
    d = split3(jnp.full((8, rows), same - other, F32))
    o = split3(jnp.full((8, rows), other, F32))
    picked = jnp.concatenate([d[0].astype(F32), d[1].astype(F32), d[2].astype(F32)], axis=0)
    eight = sub[:8, :]
    tail = jnp.where(eight == 0, o[0].astype(F32), jnp.where(eight == 1, o[1].astype(F32), jnp.where(eight == 2, o[2].astype(F32), jnp.where(eight == 3, 1.0, 0.0))))
    top = jnp.where(hit[:24], picked, 0.0)
    return jnp.concatenate([top.astype(BF16), tail.astype(BF16), jnp.zeros((96, rows), BF16)], axis=0)


def attend(q, k_ref, vt_ref, terms, bias_ref, head, variate):
    pair = head // 2
    rows = q.shape[1]
    zero = jnp.zeros((HD, rows), BF16)
    q_head = q[head * HD : (head + 1) * HD, :]
    both = [q_head, zero] if head % 2 == 0 else [zero, q_head]
    q_cat = jnp.concatenate(both + [row_terms(bias_ref, head, variate)], axis=0)
    k_cat = jnp.concatenate([k_ref[:, pair * 128 : (pair + 1) * 128], terms], axis=1)
    scores = jnp.dot(k_cat, q_cat, preferred_element_type=F32)
    peak = jnp.max(scores, axis=0, keepdims=True)
    weights = jnp.exp(scores - peak)
    total = jnp.sum(weights, axis=0, keepdims=True)
    mixed = jnp.dot(vt_ref[head * HD : (head + 1) * HD, :], weights.astype(BF16), preferred_element_type=F32)
    return (mixed / total).astype(BF16), peak + jnp.log(total)


def first_kernel(code_ref, bias_ref, k_ref, vt_ref, *refs):
    msgs, (o_ref, lse_ref) = refs[:-2], refs[-2:]
    heads = k_ref.shape[1] // HD
    cols = heads * HD
    terms = slot_terms(code_ref)
    for b, msg in enumerate(msgs):
        variate = msg[cols : cols + AUX, :].astype(F32)[0:1, :].astype(I32)
        q = msg[:cols, :]
        for head in range(heads):
            o, lse = attend(q, k_ref, vt_ref, terms, bias_ref, head, variate)
            o_ref[b, head * HD : (head + 1) * HD, :] = o
            lse_ref[b, head : head + 1, :] = lse


def second_kernel(ids_ref, code_ref, bias_ref, k_ref, vt_ref, o_ref, lse_ref, *refs):
    count = len(refs) // 2
    msgs, outs = refs[:count], refs[count:]
    heads = k_ref.shape[1] // HD
    cols = heads * HD
    terms = slot_terms(code_ref)
    for b, (msg, out) in enumerate(zip(msgs, outs)):
        aux = msg[cols : cols + AUX, :].astype(F32).astype(I32)
        variate = aux[0:1, :]
        paths = aux[1:4, :]
        mine = jnp.max((paths == ids_ref[0]).astype(I32), axis=0, keepdims=True) > 0
        theirs = jnp.max((paths == ids_ref[1]).astype(I32), axis=0, keepdims=True) > 0
        q = msg[:cols, :]
        merged = []
        for head in range(heads):
            o2, lse2 = attend(q, k_ref, vt_ref, terms, bias_ref, head, variate)
            lse2 = jnp.where(theirs, lse2, FAR)
            lse1 = jnp.where(mine, lse_ref[b, head : head + 1, :], FAR)
            top = jnp.maximum(lse1, lse2)
            w1, w2 = jnp.exp(lse1 - top), jnp.exp(lse2 - top)
            o1 = o_ref[b, head * HD : (head + 1) * HD, :].astype(F32)
            out[head * HD : (head + 1) * HD, :] = ((w1 * o1 + w2 * o2.astype(F32)) / (w1 + w2)).astype(BF16)
            merged.append(top + jnp.log(w1 + w2))
        pieces = [piece.astype(F32) for lse in merged for piece in split3(lse)]
        pieces.append(jnp.zeros((AUX - 3 * heads, variate.shape[1]), F32))
        out[cols:, :] = jnp.concatenate(pieces, axis=0).astype(BF16)


def combine_kernel(bias_ref, q_ref, k_ref, v_ref, *refs):
    parts, attn_ref = refs[:-1], refs[-1]
    cols = k_ref.shape[0]
    heads = cols // HD
    auxes = [part[cols:, :].astype(F32) for part in parts]
    done = []
    for head in range(heads):
        at = slice(head * HD, (head + 1) * HD)
        q, k = q_ref[at, :].astype(F32), k_ref[at, :].astype(F32)
        own = jnp.sum(q * k, axis=0, keepdims=True) + bias_ref[1, head]
        lses = [sum(aux[3 * head + i : 3 * head + i + 1, :] for i in range(3)) for aux in auxes]
        top = own
        for lse in lses:
            top = jnp.maximum(top, lse)
        weight = jnp.exp(own - top)
        whole = weight
        acc = weight * v_ref[at, :].astype(F32)
        for lse, part in zip(lses, parts):
            weight = jnp.exp(lse - top)
            whole = whole + weight
            acc = acc + weight * part[at, :].astype(F32)
        done.append(acc / whole)
    attn_ref[...] = jnp.concatenate(done, axis=0).T.astype(BF16)


def project_kernel(tok_ref, *refs):
    out_ref = refs[-1]
    half = (len(refs) - 1) // 2
    total = tok_ref[...].astype(F32)
    acc = None
    for attn, w in zip(refs[:half], refs[half : 2 * half]):
        term = jnp.dot(attn[...], w[...], preferred_element_type=F32)
        acc = term if acc is None else acc + term
    out_ref[...] = (total + acc).astype(BF16)


def xor(axis, k):
    return [(i, i ^ k) for i in range(lax.axis_size(axis))]


def dense_body(
    tokens,
    norm_gain,
    w_qkv,
    w_out,
    head_bias,
    kv_pool,
    key_variate,
    page_table,
    node_len,
    path_nodes,
    query_variate,
):
    rows, width = tokens.shape
    cols = w_qkv.shape[2]
    heads = cols // HD
    pages, page = key_variate.shape
    slots = pages * page
    owners, parts = lax.axis_size("seq"), lax.axis_size("tp")
    groups = [2 * k for k in range(owners // 2)]

    place = jnp.sum(jnp.where(page_table[0][:, None] == jnp.arange(pages)[None, :], jnp.arange(pages)[:, None], 0), axis=0)
    valid = place[:, None] * page + jnp.arange(page)[None, :] < node_len[0]
    code = jnp.where(valid, key_variate, 8).astype(I32)
    pool = kv_pool.reshape(slots, 2, cols)
    keys = pool[:, 0]
    values_t = pool[:, 1].T
    keys2 = lax.ppermute(keys, "seq", xor("seq", 1))
    values2 = lax.ppermute(values_t, "seq", xor("seq", 1))
    code2 = lax.ppermute(code, "seq", xor("seq", 1))

    aux = jnp.concatenate([query_variate[None], path_nodes.T, jnp.zeros((AUX - 4, rows), I32)], axis=0).astype(BF16)
    msg, normed = call(
        query_kernel,
        [shape(cols + AUX, rows), shape(rows, width)],
        tokens, norm_gain[None], w_qkv[:, 0], aux,
        flops=2 * rows * width * cols,
    )
    msgs = [msg] + [lax.ppermute(msg, "seq", xor("seq", k)) for k in groups[1:]]

    outs = [w_out]
    outs.append(lax.ppermute(w_out, "tp", xor("tp", 2)))
    outs += [lax.ppermute(w, "tp", xor("tp", 1)) for w in outs[:2]]

    key, value = call(own_kernel, [shape(cols, rows)] * 2, normed, w_qkv[:, 1], w_qkv[:, 2], flops=4 * rows * width * cols)

    work = 4 * len(groups) * rows * slots * cols
    o1, lse1 = call(
        first_kernel,
        [shape(len(groups), cols, rows), shape(len(groups), heads, rows, dtype=F32)],
        code, head_bias, keys, values_t, *msgs,
        flops=work,
    )
    me = lax.axis_index("seq")
    ids = jnp.stack([me, me ^ 1]).astype(I32)
    merged = call(
        second_kernel,
        [shape(cols + AUX, rows)] * len(groups),
        ids, code2, head_bias, keys2, values2, o1, lse1, *msgs,
        flops=work,
    )
    back = [merged[0]] + [lax.ppermute(m, "seq", xor("seq", k)) for m, k in zip(merged[1:], groups[1:])]
    attn = call(combine_kernel, shape(rows, cols), head_bias, msg, key, value, *back)
    attns = [attn] + [lax.ppermute(attn, "tp", xor("tp", k)) for k in (2, 1, 3)]
    return call(project_kernel, shape(rows, width), tokens, *attns, *outs, flops=2 * rows * width * width)


def solution(mesh):
    in_specs = (
        P("seq", None),
        P(),
        P(None, None, "tp"),
        P("tp", None),
        P(None, "tp"),
        P("seq", None, None, "tp"),
        P("seq", None),
        P("seq", None),
        P("seq"),
        P("seq", None),
        P("seq"),
    )
    out_specs = P("seq", None)
    dense = mesh.shape["seq"] == 8 and mesh.shape["tp"] == 4
    body = dense_body if dense else routed_body
    return jax.shard_map(body, mesh=mesh, in_specs=in_specs, out_specs=out_specs, check_vma=False)
```

```python
import jax
import jax.numpy as jnp
from jax import lax
from jax.experimental import pallas as pl
from jax.experimental.pallas import tpu as pltpu
from jax.sharding import PartitionSpec as P

HD = 64


def head_attend(qh, kh, vh, same, bias_same, bias_diff, valid):
    scores = jnp.dot(qh, kh.T, preferred_element_type=jnp.float32) * HD ** (-0.5)
    scores = scores + jnp.where(same, bias_same, bias_diff)
    scores = jnp.where(valid[None, :], scores, -1e30)
    peak = jnp.max(scores, axis=1)
    weights = jnp.exp(scores - peak[:, None])
    total = jnp.sum(weights, axis=1)
    mixed = (
        jnp.dot(weights.astype(jnp.bfloat16), vh, preferred_element_type=jnp.float32)
        / total[:, None]
    )
    mixed = lax.optimization_barrier(mixed.astype(jnp.bfloat16))
    return (mixed, peak, total)


def place_rows(dest, values, variates, owners, slots):
    onehot = (dest[:, None] == jnp.arange(owners, dtype=jnp.int32)[None, :]).astype(jnp.int32)
    before = jnp.cumsum(onehot, axis=0) - onehot
    slot = jnp.sum(before * onehot, axis=1)
    flat = dest * slots + slot
    width = values.shape[1]
    qbuf = (
        jnp.zeros((owners * slots, width), jnp.bfloat16)
        .at[flat]
        .set(values)
        .reshape(owners, slots, width)
    )
    vbuf = jnp.zeros((owners * slots,), jnp.int32).at[flat].set(variates).reshape(owners, slots)
    return (qbuf, vbuf, flat)


def routed_body(
    tokens,
    norm_gain,
    w_qkv,
    w_out,
    head_bias,
    kv_pool,
    key_variate,
    page_table,
    node_len,
    path_nodes,
    query_variate,
):
    tok_rows, width = tokens.shape
    heads_here = w_qkv.shape[2] // HD
    owners = lax.axis_size("seq")
    slots = min(tok_rows, 8 * tok_rows // owners)
    xf = tokens.astype(jnp.float32)
    normed = (xf * lax.rsqrt(jnp.mean(xf * xf, axis=1, keepdims=True) + 1e-05) * norm_gain).astype(
        jnp.bfloat16
    )
    qkv = jnp.dot(
        normed, w_qkv.reshape(width, 3 * heads_here * HD), preferred_element_type=jnp.float32
    ).astype(jnp.bfloat16)
    qkv = qkv.reshape(tok_rows, 3, heads_here, HD)
    query, key, value = (qkv[:, 0], qkv[:, 1], qkv[:, 2])
    order = page_table[0]
    node_slots = kv_pool.shape[0] * kv_pool.shape[1]
    pages = kv_pool[order].reshape(node_slots, 2, heads_here, HD)
    node_keys = jnp.moveaxis(pages[:, 0], 1, 0)
    node_values = jnp.moveaxis(pages[:, 1], 1, 0)
    key_var = key_variate[order].reshape(node_slots)
    valid = jnp.arange(node_slots, dtype=jnp.int32) < node_len[0]
    qflat = query.reshape(tok_rows, heads_here * HD)
    out_list, peak_list, total_list = ([], [], [])
    for level in range(3):
        qbuf, vbuf, flat = place_rows(path_nodes[:, level], qflat, query_variate, owners, slots)
        owner_qbuf = lax.all_to_all(qbuf, "seq", split_axis=0, concat_axis=0, tiled=True)
        owner_vbuf = lax.all_to_all(vbuf, "seq", split_axis=0, concat_axis=0, tiled=True)
        sources, count, cols = owner_qbuf.shape
        rows = sources * count
        heads_q = jnp.moveaxis(owner_qbuf.reshape(rows, heads_here, HD), 1, 0)
        same = owner_vbuf.reshape(rows)[:, None] == key_var[None, :]

        def per_head(xs):
            return head_attend(xs[0], xs[1], xs[2], same, xs[3], xs[4], valid)

        mixed, peak, total = lax.map(
            per_head, (heads_q, node_keys, node_values, head_bias[1], head_bias[0])
        )
        mixed = jnp.moveaxis(mixed, 0, 1).reshape(sources, count, cols)
        peak = peak.T.reshape(sources, count, heads_here)
        total = total.T.reshape(sources, count, heads_here)
        mixed_back = lax.all_to_all(mixed, "seq", split_axis=0, concat_axis=0, tiled=True)
        peak_back = lax.all_to_all(peak, "seq", split_axis=0, concat_axis=0, tiled=True)
        total_back = lax.all_to_all(total, "seq", split_axis=0, concat_axis=0, tiled=True)
        mixed = mixed_back
        peak = peak_back
        total = total_back
        out_list.append(mixed.reshape(owners * slots, -1)[flat].reshape(tok_rows, heads_here, HD))
        peak_list.append(peak.reshape(owners * slots, heads_here)[flat])
        total_list.append(total.reshape(owners * slots, heads_here)[flat])
    outs = jnp.stack(out_list, axis=1)
    peaks = jnp.stack(peak_list, axis=1)
    totals = jnp.stack(total_list, axis=1)
    own_peak = (
        jnp.sum(query.astype(jnp.float32) * key.astype(jnp.float32), axis=2) * HD ** (-0.5)
        + head_bias[1][None, :]
    )
    all_o = jnp.concatenate([value.astype(jnp.float32)[:, None], outs.astype(jnp.float32)], axis=1)
    all_m = jnp.concatenate([own_peak[:, None], peaks], axis=1)
    all_l = jnp.concatenate([jnp.ones((tok_rows, 1, heads_here), jnp.float32), totals], axis=1)
    top = jnp.max(all_m, axis=1, keepdims=True)
    scale = all_l * jnp.exp(all_m - top)
    attn = (jnp.sum(scale[..., None] * all_o, axis=1) / jnp.sum(scale, axis=1)[..., None]).astype(
        jnp.bfloat16
    )
    partial_sum = jnp.dot(
        attn.reshape(tok_rows, heads_here * HD), w_out, preferred_element_type=jnp.float32
    )
    total_sum = lax.psum(partial_sum, "tp")
    return (xf + total_sum).astype(jnp.bfloat16)


BF16, F32, I32 = jnp.bfloat16, jnp.float32, jnp.int32
AUX = 16
FAR = -1e30
VMEM = pl.BlockSpec(memory_space=pltpu.VMEM)
HBM = pl.BlockSpec(memory_space=pltpu.HBM)
SMEM = pl.BlockSpec(memory_space=pltpu.SMEM)


def call(kernel, outs, *args, flops=1, away=(), scratch=(), grant=16):
    single = not isinstance(outs, (tuple, list))
    args = [pltpu.with_memory_space_constraint(a, pltpu.HBM) if i in away else a for i, a in enumerate(args)]
    return pl.pallas_call(
        kernel,
        out_shape=outs,
        scratch_shapes=scratch,
        in_specs=[HBM if i in away else SMEM if a.size == 1 else VMEM for i, a in enumerate(args)],
        out_specs=VMEM if single else [VMEM] * len(outs),
        compiler_params=pltpu.CompilerParams(vmem_limit_bytes=grant << 20),
        cost_estimate=pl.CostEstimate(flops=1, bytes_accessed=1, transcendentals=0),
    )(*args)


def shape(*dims, dtype=BF16):
    return jax.ShapeDtypeStruct(dims, dtype)


def fetch(sems, *pairs):
    copies = [pltpu.make_async_copy(src, dst, sems.at[i]) for i, (src, dst) in enumerate(pairs)]
    for copy in copies:
        copy.start()
    return copies


def query_kernel(
    tok_hbm, gain_hbm, w_hbm, variate_hbm, path_hbm, bias_hbm, slot_hbm, table_hbm, len_ref,
    msg_ref, normed_ref, rows_ref, code_ref, tok_ref,
    gain_ref, w_ref, variate_ref, path_ref, bias_ref, slot_ref, table_ref, sems,
):
    copies = fetch(
        sems, (tok_hbm, tok_ref), (w_hbm.at[0], w_ref), (gain_hbm, gain_ref), (variate_hbm, variate_ref), (path_hbm, path_ref),
        (bias_hbm, bias_ref), (slot_hbm, slot_ref), (table_hbm, table_ref),
    )
    for copy in copies[2:]:
        copy.wait()
    pages, page = slot_ref.shape
    length = len_ref[0]
    offset = lax.broadcasted_iota(I32, (1, page), 1)
    for p in range(pages):
        place = sum(jnp.where(table_ref[0, i] == p, i, 0) for i in range(pages))
        code_ref[p : p + 1, :] = jnp.where(place * page + offset < length, slot_ref[p : p + 1, :], 8)
    rows, cols = tok_ref.shape[0], w_ref.shape[1]
    for head in range(cols // HD):
        same = jnp.full((1, rows), bias_ref[1, head], F32)
        other = jnp.full((1, rows), bias_ref[0, head], F32)
        rows_ref[8 * head : 8 * head + 8, :] = jnp.concatenate([same, other, same - other, jnp.zeros((5, rows), F32)], axis=0)
    aux = [variate_ref[...].astype(F32), path_ref[...].astype(F32), jnp.zeros((AUX - 4, rows), F32)]
    msg_ref[cols:, :] = jnp.concatenate(aux, axis=0).astype(BF16)
    copies[0].wait()
    x = tok_ref[...].astype(F32)
    r = lax.rsqrt(jnp.mean(x * x, axis=1, keepdims=True) + 1e-05)
    normed = (x * r * gain_ref[...]).astype(BF16)
    normed_ref[...] = normed
    copies[1].wait()
    q = jnp.dot(normed, w_ref[...], preferred_element_type=F32).astype(BF16)
    msg_ref[:cols, :] = (q.astype(F32) * HD ** (-0.5)).T.astype(BF16)


def split3(x):
    a = x.astype(BF16).astype(F32)
    b = (x - a).astype(BF16).astype(F32)
    return a, b, (x - a - b).astype(BF16).astype(F32)


def split_pool(pool_ref):
    slots, _, cols = pool_ref.shape
    i = lax.broadcasted_iota(I32, (256, 256), 0)
    j = lax.broadcasted_iota(I32, (256, 256), 1)
    pick = jnp.where(j == 2 * (i % 128) + i // 128, 1.0, 0.0).astype(BF16)
    keys, values = [], []
    for at in range(0, slots, 128):
        both = pool_ref[at : at + 128].reshape(256, cols)
        apart = jnp.dot(pick, both, preferred_element_type=F32)
        keys.append(apart[:128].astype(BF16))
        values.append(apart[128:].T.astype(BF16))
    return jnp.concatenate(keys, axis=0), jnp.concatenate(values, axis=1)


def slot_terms(code_ref):
    pages, page = code_ref.shape
    sub = lax.broadcasted_iota(I32, (128, page), 0)
    blocks = []
    for p in range(pages):
        code = jnp.broadcast_to(code_ref[p : p + 1, :], (128, page))
        hit = ((code == sub % 8) & (sub < 24)) | ((sub >= 24) & (sub < 27))
        term = jnp.where(hit, 1.0, 0.0)
        term = jnp.where((sub == 27) & (code == 8), FAR, term)
        blocks.append(term.T.astype(BF16))
    return jnp.concatenate(blocks, axis=0)


def row_terms(bias, variate):
    rows = variate.shape[1]
    sub = lax.broadcasted_iota(I32, (8, rows), 0)
    hit = variate == sub
    other, step = split3(bias[1:2, :]), split3(bias[2:3, :])
    picked = [jnp.where(hit, jnp.broadcast_to(piece, (8, rows)), 0.0) for piece in step]
    tail = jnp.where(sub == 3, 1.0, 0.0)
    for at, piece in enumerate(other):
        tail = jnp.where(sub == at, piece, tail)
    top = jnp.concatenate(picked + [tail], axis=0).astype(BF16)
    return jnp.concatenate([top, jnp.zeros((96, rows), BF16)], axis=0)


def attend(q, keys, values_t, terms, bias, variate, head):
    pair = head // 2
    q_head = q[head * HD : (head + 1) * HD, :]
    zero = jnp.zeros_like(q_head)
    both = [q_head, zero] if head % 2 == 0 else [zero, q_head]
    q_cat = jnp.concatenate(both + [row_terms(bias, variate)], axis=0)
    k_cat = jnp.concatenate([keys[:, pair * 128 : (pair + 1) * 128], terms], axis=1)
    scores = jnp.dot(k_cat, q_cat, preferred_element_type=F32)
    peak = jnp.max(scores, axis=0, keepdims=True)
    weights = jnp.exp(scores - peak)
    total = jnp.sum(weights, axis=0, keepdims=True)
    mixed = jnp.dot(values_t[head * HD : (head + 1) * HD, :], weights.astype(BF16), preferred_element_type=F32)
    return (mixed / total).astype(BF16), peak + jnp.log(total)


def wide(rows_ref, head, blocks):
    return jnp.concatenate([rows_ref[8 * head : 8 * head + 8, :]] * blocks, axis=1)


def gather_rows(msgs, cols):
    q = jnp.concatenate([msg[:cols, :] for msg in msgs], axis=1)
    aux = jnp.concatenate([msg[cols:, :].astype(F32).astype(I32) for msg in msgs], axis=1)
    return q, aux


def own_kernel(normed_ref, w_ref, k_ref, v_ref):
    for i, own_ref in ((1, k_ref), (2, v_ref)):
        own = jnp.dot(normed_ref[...], w_ref[i], preferred_element_type=F32).astype(BF16)
        own_ref[...] = own.astype(F32).T.astype(BF16)


def first_kernel(rows_ref, pool_ref, code_ref, *refs):
    msgs, (o_ref, lse_ref) = refs[:-2], refs[-2:]
    keys, values_t = split_pool(pool_ref)
    terms = slot_terms(code_ref)
    cols = keys.shape[1]
    q, aux = gather_rows(msgs, cols)
    for head in range(cols // HD):
        o, lse = attend(q, keys, values_t, terms, wide(rows_ref, head, len(msgs)), aux[0:1, :], head)
        o_ref[head * HD : (head + 1) * HD, :] = o
        lse_ref[head : head + 1, :] = lse


def second_kernel(rows_ref, pool_ref, code_ref, o_ref, lse_ref, *refs):
    count = len(refs) // 2
    msgs, outs = refs[:count], refs[count:]
    keys, values_t = split_pool(pool_ref)
    cols = keys.shape[1]
    heads = cols // HD
    rows = msgs[0].shape[1]
    terms = slot_terms(code_ref)
    q, aux = gather_rows(msgs, cols)
    me = lax.axis_index("seq")
    named = lambda node: jnp.max((aux[1:4, :] == node).astype(I32), axis=0, keepdims=True) > 0
    mine, theirs = named(me), named(me ^ 1)
    pieces = []
    for head in range(heads):
        o2, lse2 = attend(q, keys, values_t, terms, wide(rows_ref, head, count), aux[0:1, :], head)
        lse2 = jnp.where(theirs, lse2, FAR)
        lse1 = jnp.where(mine, lse_ref[head : head + 1, :], FAR)
        top = jnp.maximum(lse1, lse2)
        w1, w2 = jnp.exp(lse1 - top), jnp.exp(lse2 - top)
        o1 = o_ref[head * HD : (head + 1) * HD, :].astype(F32)
        merged = ((w1 * o1 + w2 * o2.astype(F32)) / (w1 + w2)).astype(BF16)
        for b, out in enumerate(outs):
            out[head * HD : (head + 1) * HD, :] = merged[:, b * rows : (b + 1) * rows]
        pieces += split3(top + jnp.log(w1 + w2))
    pieces.append(jnp.zeros((AUX - 3 * heads, count * rows), F32))
    tail = jnp.concatenate(pieces, axis=0).astype(BF16)
    for b, out in enumerate(outs):
        out[cols:, :] = tail[:, b * rows : (b + 1) * rows]


def combine_kernel(rows_ref, q_ref, k_ref, v_ref, *refs):
    parts, attn_ref = refs[:-1], refs[-1]
    cols = k_ref.shape[0]
    auxes = [part[cols:, :].astype(F32) for part in parts]
    done = []
    for head in range(cols // HD):
        at = slice(head * HD, (head + 1) * HD)
        q, k = q_ref[at, :].astype(F32), k_ref[at, :].astype(F32)
        own = jnp.sum(q * k, axis=0, keepdims=True) + rows_ref[8 * head : 8 * head + 1, :]
        lses = [sum(aux[3 * head + i : 3 * head + i + 1, :] for i in range(3)) for aux in auxes]
        top = own
        for lse in lses:
            top = jnp.maximum(top, lse)
        weight = jnp.exp(own - top)
        whole = weight
        acc = weight * v_ref[at, :].astype(F32)
        for lse, part in zip(lses, parts):
            weight = jnp.exp(lse - top)
            whole = whole + weight
            acc = acc + weight * part[at, :].astype(F32)
        done.append(acc / whole)
    attn_ref[...] = jnp.concatenate(done, axis=0).T.astype(BF16)


def project_kernel(tok_ref, *refs):
    out_ref = refs[-1]
    half = (len(refs) - 1) // 2
    acc = None
    for attn, w in zip(refs[:half], refs[half : 2 * half]):
        term = jnp.dot(attn[...], w[...], preferred_element_type=F32)
        acc = term if acc is None else acc + term
    out_ref[...] = (tok_ref[...].astype(F32) + acc).astype(BF16)


def xor(axis, k):
    return [(i, i ^ k) for i in range(lax.axis_size(axis))]


def dense_body(
    tokens,
    norm_gain,
    w_qkv,
    w_out,
    head_bias,
    kv_pool,
    key_variate,
    page_table,
    node_len,
    path_nodes,
    query_variate,
):
    rows, width = tokens.shape
    cols = w_qkv.shape[2]
    heads = cols // HD
    pages, page = key_variate.shape
    slots = pages * page
    groups = [2 * k for k in range(max(1, lax.axis_size("seq") // 2))]

    pool = kv_pool.reshape(slots, 2, cols)
    pool2 = lax.ppermute(pool, "seq", xor("seq", 1))

    w3 = w_qkv.transpose(1, 0, 2)
    smem = lambda *dims: pltpu.SMEM(dims, I32)
    msg, normed, bias, code, tok = call(
        query_kernel,
        [
            shape(cols + AUX, rows),
            shape(rows, width),
            shape(8 * heads, rows, dtype=F32),
            shape(pages, page, dtype=I32),
            shape(rows, width),
        ],
        tokens, norm_gain[None], w3, query_variate[None], path_nodes.T, head_bias, key_variate, page_table, node_len,
        flops=2 * rows * width * cols,
        away=range(8),
        scratch=[
            pltpu.VMEM((1, width), F32), pltpu.VMEM((width, cols), BF16), pltpu.VMEM((1, rows), I32), pltpu.VMEM((3, rows), I32),
            pltpu.VMEM((2, heads), F32), pltpu.VMEM((pages, page), I32), smem(1, pages), pltpu.SemaphoreType.DMA((8,)),
        ],
    )
    code2 = lax.ppermute(code, "seq", xor("seq", 1))
    msgs = [msg] + [lax.ppermute(msg, "seq", xor("seq", k)) for k in groups[1:]]

    w_own, *msgs = lax.optimization_barrier((w_out, *msgs))
    w_far = lax.ppermute(w_own, "tp", xor("tp", 2))

    work = 4 * len(groups) * rows * slots * cols
    wide_rows = len(groups) * rows
    o1, lse1 = call(
        first_kernel,
        [shape(cols, wide_rows), shape(heads, wide_rows, dtype=F32)],
        bias, pool, code, *msgs,
        flops=work,
    )
    merged = call(
        second_kernel, [shape(cols + AUX, rows)] * len(groups), bias, pool2, code2, o1, lse1, *msgs, flops=work)
    first, w_own, w_far, normed = lax.optimization_barrier((merged[0], w_own, w_far, normed))
    key, value = call(own_kernel, [shape(cols, rows)] * 2, normed, w3, flops=4 * rows * width * cols)
    outs = [w_own, w_far] + [lax.ppermute(w, "tp", xor("tp", 1)) for w in (w_own, w_far)]
    back = [first] + [lax.ppermute(m, "seq", xor("seq", k)) for m, k in zip(merged[1:], groups[1:])]
    attn = call(combine_kernel, shape(rows, cols), bias, msg, key, value, *back)
    attns = [attn] + [lax.ppermute(attn, "tp", xor("tp", k)) for k in (2, 1, 3)]
    return call(project_kernel, shape(rows, width), tok, *attns, *outs, flops=2 * rows * width * width)


def solution(mesh):
    in_specs = (
        P("seq", None),
        P(),
        P(None, None, "tp"),
        P("tp", None),
        P(None, "tp"),
        P("seq", None, None, "tp"),
        P("seq", None),
        P("seq", None),
        P("seq"),
        P("seq", None),
        P("seq"),
    )
    out_specs = P("seq", None)
    owners, parts = mesh.shape["seq"], mesh.shape["tp"]
    dense = owners <= 8 and owners & (owners - 1) == 0 and parts == 4
    body = dense_body if dense else routed_body
    return jax.shard_map(body, mesh=mesh, in_specs=in_specs, out_specs=out_specs, check_vma=False)
```

```python
import jax
import jax.numpy as jnp
from jax import lax
from jax.experimental import pallas as pl
from jax.experimental.pallas import tpu as pltpu
from jax.sharding import PartitionSpec as P

HD = 64


def head_attend(qh, kh, vh, same, bias_same, bias_diff, valid):
    scores = jnp.dot(qh, kh.T, preferred_element_type=jnp.float32) * HD ** (-0.5)
    scores = scores + jnp.where(same, bias_same, bias_diff)
    scores = jnp.where(valid[None, :], scores, -1e30)
    peak = jnp.max(scores, axis=1)
    weights = jnp.exp(scores - peak[:, None])
    total = jnp.sum(weights, axis=1)
    mixed = (
        jnp.dot(weights.astype(jnp.bfloat16), vh, preferred_element_type=jnp.float32)
        / total[:, None]
    )
    mixed = lax.optimization_barrier(mixed.astype(jnp.bfloat16))
    return (mixed, peak, total)


def place_rows(dest, values, variates, owners, slots):
    onehot = (dest[:, None] == jnp.arange(owners, dtype=jnp.int32)[None, :]).astype(jnp.int32)
    before = jnp.cumsum(onehot, axis=0) - onehot
    slot = jnp.sum(before * onehot, axis=1)
    flat = dest * slots + slot
    width = values.shape[1]
    qbuf = (
        jnp.zeros((owners * slots, width), jnp.bfloat16)
        .at[flat]
        .set(values)
        .reshape(owners, slots, width)
    )
    vbuf = jnp.zeros((owners * slots,), jnp.int32).at[flat].set(variates).reshape(owners, slots)
    return (qbuf, vbuf, flat)


def routed_body(
    tokens,
    norm_gain,
    w_qkv,
    w_out,
    head_bias,
    kv_pool,
    key_variate,
    page_table,
    node_len,
    path_nodes,
    query_variate,
):
    tok_rows, width = tokens.shape
    heads_here = w_qkv.shape[2] // HD
    owners = lax.axis_size("seq")
    slots = min(tok_rows, 8 * tok_rows // owners)
    xf = tokens.astype(jnp.float32)
    normed = (xf * lax.rsqrt(jnp.mean(xf * xf, axis=1, keepdims=True) + 1e-05) * norm_gain).astype(
        jnp.bfloat16
    )
    qkv = jnp.dot(
        normed, w_qkv.reshape(width, 3 * heads_here * HD), preferred_element_type=jnp.float32
    ).astype(jnp.bfloat16)
    qkv = qkv.reshape(tok_rows, 3, heads_here, HD)
    query, key, value = (qkv[:, 0], qkv[:, 1], qkv[:, 2])
    order = page_table[0]
    node_slots = kv_pool.shape[0] * kv_pool.shape[1]
    pages = kv_pool[order].reshape(node_slots, 2, heads_here, HD)
    node_keys = jnp.moveaxis(pages[:, 0], 1, 0)
    node_values = jnp.moveaxis(pages[:, 1], 1, 0)
    key_var = key_variate[order].reshape(node_slots)
    valid = jnp.arange(node_slots, dtype=jnp.int32) < node_len[0]
    qflat = query.reshape(tok_rows, heads_here * HD)
    out_list, peak_list, total_list = ([], [], [])
    for level in range(3):
        qbuf, vbuf, flat = place_rows(path_nodes[:, level], qflat, query_variate, owners, slots)
        owner_qbuf = lax.all_to_all(qbuf, "seq", split_axis=0, concat_axis=0, tiled=True)
        owner_vbuf = lax.all_to_all(vbuf, "seq", split_axis=0, concat_axis=0, tiled=True)
        sources, count, cols = owner_qbuf.shape
        rows = sources * count
        heads_q = jnp.moveaxis(owner_qbuf.reshape(rows, heads_here, HD), 1, 0)
        same = owner_vbuf.reshape(rows)[:, None] == key_var[None, :]

        def per_head(xs):
            return head_attend(xs[0], xs[1], xs[2], same, xs[3], xs[4], valid)

        mixed, peak, total = lax.map(
            per_head, (heads_q, node_keys, node_values, head_bias[1], head_bias[0])
        )
        mixed = jnp.moveaxis(mixed, 0, 1).reshape(sources, count, cols)
        peak = peak.T.reshape(sources, count, heads_here)
        total = total.T.reshape(sources, count, heads_here)
        mixed_back = lax.all_to_all(mixed, "seq", split_axis=0, concat_axis=0, tiled=True)
        peak_back = lax.all_to_all(peak, "seq", split_axis=0, concat_axis=0, tiled=True)
        total_back = lax.all_to_all(total, "seq", split_axis=0, concat_axis=0, tiled=True)
        mixed = mixed_back
        peak = peak_back
        total = total_back
        out_list.append(mixed.reshape(owners * slots, -1)[flat].reshape(tok_rows, heads_here, HD))
        peak_list.append(peak.reshape(owners * slots, heads_here)[flat])
        total_list.append(total.reshape(owners * slots, heads_here)[flat])
    outs = jnp.stack(out_list, axis=1)
    peaks = jnp.stack(peak_list, axis=1)
    totals = jnp.stack(total_list, axis=1)
    own_peak = (
        jnp.sum(query.astype(jnp.float32) * key.astype(jnp.float32), axis=2) * HD ** (-0.5)
        + head_bias[1][None, :]
    )
    all_o = jnp.concatenate([value.astype(jnp.float32)[:, None], outs.astype(jnp.float32)], axis=1)
    all_m = jnp.concatenate([own_peak[:, None], peaks], axis=1)
    all_l = jnp.concatenate([jnp.ones((tok_rows, 1, heads_here), jnp.float32), totals], axis=1)
    top = jnp.max(all_m, axis=1, keepdims=True)
    scale = all_l * jnp.exp(all_m - top)
    attn = (jnp.sum(scale[..., None] * all_o, axis=1) / jnp.sum(scale, axis=1)[..., None]).astype(
        jnp.bfloat16
    )
    partial_sum = jnp.dot(
        attn.reshape(tok_rows, heads_here * HD), w_out, preferred_element_type=jnp.float32
    )
    total_sum = lax.psum(partial_sum, "tp")
    return (xf + total_sum).astype(jnp.bfloat16)


BF16, F32, I32 = jnp.bfloat16, jnp.float32, jnp.int32
AUX = 16
FAR = -1e30
VMEM = pl.BlockSpec(memory_space=pltpu.VMEM)
HBM = pl.BlockSpec(memory_space=pltpu.HBM)
SMEM = pl.BlockSpec(memory_space=pltpu.SMEM)


def call(kernel, outs, *args, flops=1, away=(), scratch=(), grant=16):
    single = not isinstance(outs, (tuple, list))
    args = [pltpu.with_memory_space_constraint(a, pltpu.HBM) if i in away else a for i, a in enumerate(args)]
    return pl.pallas_call(
        kernel,
        out_shape=outs,
        scratch_shapes=scratch,
        in_specs=[HBM if i in away else SMEM if a.size == 1 else VMEM for i, a in enumerate(args)],
        out_specs=VMEM if single else [VMEM] * len(outs),
        compiler_params=pltpu.CompilerParams(vmem_limit_bytes=grant << 20),
        cost_estimate=pl.CostEstimate(flops=1, bytes_accessed=1, transcendentals=0),
    )(*args)


def shape(*dims, dtype=BF16):
    return jax.ShapeDtypeStruct(dims, dtype)


def fetch(sems, *pairs):
    copies = [pltpu.make_async_copy(src, dst, sems.at[i]) for i, (src, dst) in enumerate(pairs)]
    for copy in copies:
        copy.start()
    return copies


def query_kernel(
    tok_hbm, gain_hbm, w_hbm, variate_hbm, path_hbm, bias_hbm, slot_hbm, table_hbm, len_ref,
    msg_ref, normed_ref, rows_ref, code_ref, tok_ref,
    gain_ref, w_ref, variate_ref, path_ref, bias_ref, slot_ref, table_ref, sems,
):
    copies = fetch(
        sems, (tok_hbm, tok_ref), (w_hbm.at[0], w_ref), (gain_hbm, gain_ref), (variate_hbm, variate_ref), (path_hbm, path_ref),
        (bias_hbm, bias_ref), (slot_hbm, slot_ref), (table_hbm, table_ref),
    )
    for copy in copies[2:]:
        copy.wait()
    pages, page = slot_ref.shape
    length = len_ref[0]
    offset = lax.broadcasted_iota(I32, (1, page), 1)
    for p in range(pages):
        place = sum(jnp.where(table_ref[0, i] == p, i, 0) for i in range(pages))
        code_ref[p : p + 1, :] = jnp.where(place * page + offset < length, slot_ref[p : p + 1, :], 8)
    rows, cols = tok_ref.shape[0], w_ref.shape[1]
    for head in range(cols // HD):
        same = jnp.full((1, rows), bias_ref[1, head], F32)
        other = jnp.full((1, rows), bias_ref[0, head], F32)
        rows_ref[8 * head : 8 * head + 8, :] = jnp.concatenate([same, other, same - other, jnp.zeros((5, rows), F32)], axis=0)
    aux = [variate_ref[...].astype(F32), path_ref[...].astype(F32), jnp.zeros((AUX - 4, rows), F32)]
    msg_ref[cols:, :] = jnp.concatenate(aux, axis=0).astype(BF16)
    copies[0].wait()
    x = tok_ref[...].astype(F32)
    r = lax.rsqrt(jnp.mean(x * x, axis=1, keepdims=True) + 1e-05)
    normed = (x * r * gain_ref[...]).astype(BF16)
    normed_ref[...] = normed
    copies[1].wait()
    q = jnp.dot(normed, w_ref[...], preferred_element_type=F32).astype(BF16)
    msg_ref[:cols, :] = (q.astype(F32) * HD ** (-0.5)).T.astype(BF16)


def split3(x):
    a = x.astype(BF16).astype(F32)
    b = (x - a).astype(BF16).astype(F32)
    return a, b, (x - a - b).astype(BF16).astype(F32)


def split_pool(*pool_refs):
    cols = pool_refs[0].shape[2]
    i = lax.broadcasted_iota(I32, (256, 256), 0)
    j = lax.broadcasted_iota(I32, (256, 256), 1)
    pick = jnp.where(j == 2 * (i % 128) + i // 128, 1.0, 0.0).astype(BF16)
    keys, values = [], []
    for both in [ref[at : at + 128].reshape(256, cols) for ref in pool_refs for at in range(0, ref.shape[0], 128)]:
        apart = jnp.dot(pick, both, preferred_element_type=F32)
        keys.append(apart[:128].astype(BF16))
        values.append(apart[128:].T.astype(BF16))
    return jnp.concatenate(keys, axis=0), jnp.concatenate(values, axis=1)


def slot_terms(code_ref):
    pages, page = code_ref.shape
    sub = lax.broadcasted_iota(I32, (128, page), 0)
    blocks = []
    for p in range(pages):
        code = jnp.broadcast_to(code_ref[p : p + 1, :], (128, page))
        hit = ((code == sub % 8) & (sub < 24)) | ((sub >= 24) & (sub < 27))
        term = jnp.where(hit, 1.0, 0.0)
        term = jnp.where((sub == 27) & (code == 8), FAR, term)
        blocks.append(term.T.astype(BF16))
    return jnp.concatenate(blocks, axis=0)


def row_terms(bias, variate):
    rows = variate.shape[1]
    sub = lax.broadcasted_iota(I32, (8, rows), 0)
    hit = variate == sub
    other, step = split3(bias[1:2, :]), split3(bias[2:3, :])
    picked = [jnp.where(hit, jnp.broadcast_to(piece, (8, rows)), 0.0) for piece in step]
    tail = jnp.where(sub == 3, 1.0, 0.0)
    for at, piece in enumerate(other):
        tail = jnp.where(sub == at, piece, tail)
    top = jnp.concatenate(picked + [tail], axis=0).astype(BF16)
    return jnp.concatenate([top, jnp.zeros((96, rows), BF16)], axis=0)


def attend(q, keys, values_t, terms, bias, variate, head):
    pair = head // 2
    q_head = q[head * HD : (head + 1) * HD, :]
    zero = jnp.zeros_like(q_head)
    both = [q_head, zero] if head % 2 == 0 else [zero, q_head]
    q_cat = jnp.concatenate(both + [row_terms(bias, variate)], axis=0)
    k_cat = jnp.concatenate([keys[:, pair * 128 : (pair + 1) * 128], terms], axis=1)
    scores = jnp.dot(k_cat, q_cat, preferred_element_type=F32)
    peak = jnp.max(scores, axis=0, keepdims=True)
    weights = jnp.exp(scores - peak)
    total = jnp.sum(weights, axis=0, keepdims=True)
    mixed = jnp.dot(values_t[head * HD : (head + 1) * HD, :], weights.astype(BF16), preferred_element_type=F32)
    return (mixed / total).astype(BF16), peak + jnp.log(total)


def wide(rows_ref, head, blocks):
    return jnp.concatenate([rows_ref[8 * head : 8 * head + 8, :]] * blocks, axis=1)


def gather_rows(msgs, cols):
    q = jnp.concatenate([msg[:cols, :] for msg in msgs], axis=1)
    aux = jnp.concatenate([msg[cols:, :].astype(F32).astype(I32) for msg in msgs], axis=1)
    return q, aux


def own_kernel(normed_ref, w_ref, k_ref, v_ref):
    for i, own_ref in ((1, k_ref), (2, v_ref)):
        own = jnp.dot(normed_ref[...], w_ref[i], preferred_element_type=F32).astype(BF16)
        own_ref[...] = own.astype(F32).T.astype(BF16)


def first_kernel(rows_ref, pool_ref, code_ref, *refs):
    msgs, (o_ref, lse_ref) = refs[:-2], refs[-2:]
    keys, values_t = split_pool(pool_ref)
    terms = slot_terms(code_ref)
    cols = keys.shape[1]
    q, aux = gather_rows(msgs, cols)
    for head in range(cols // HD):
        o, lse = attend(q, keys, values_t, terms, wide(rows_ref, head, len(msgs)), aux[0:1, :], head)
        o_ref[head * HD : (head + 1) * HD, :] = o
        lse_ref[head : head + 1, :] = lse


def second_kernel(rows_ref, pool_ref, code_ref, o_ref, lse_ref, *refs):
    count = len(refs) // 2
    msgs, outs = refs[:count], refs[count:]
    keys, values_t = split_pool(pool_ref)
    cols = keys.shape[1]
    heads = cols // HD
    rows = msgs[0].shape[1]
    terms = slot_terms(code_ref)
    q, aux = gather_rows(msgs, cols)
    me = lax.axis_index("seq")
    named = lambda node: jnp.max((aux[1:4, :] == node).astype(I32), axis=0, keepdims=True) > 0
    mine, theirs = named(me), named(me ^ 1)
    pieces = []
    for head in range(heads):
        o2, lse2 = attend(q, keys, values_t, terms, wide(rows_ref, head, count), aux[0:1, :], head)
        lse2 = jnp.where(theirs, lse2, FAR)
        lse1 = jnp.where(mine, lse_ref[head : head + 1, :], FAR)
        top = jnp.maximum(lse1, lse2)
        w1, w2 = jnp.exp(lse1 - top), jnp.exp(lse2 - top)
        o1 = o_ref[head * HD : (head + 1) * HD, :].astype(F32)
        merged = ((w1 * o1 + w2 * o2.astype(F32)) / (w1 + w2)).astype(BF16)
        for b, out in enumerate(outs):
            out[head * HD : (head + 1) * HD, :] = merged[:, b * rows : (b + 1) * rows]
        pieces += split3(top + jnp.log(w1 + w2))
    pieces.append(jnp.zeros((AUX - 3 * heads, count * rows), F32))
    tail = jnp.concatenate(pieces, axis=0).astype(BF16)
    for b, out in enumerate(outs):
        out[cols:, :] = tail[:, b * rows : (b + 1) * rows]


def combine_kernel(rows_ref, q_ref, k_ref, v_ref, *refs):
    parts, attn_ref = refs[:-1], refs[-1]
    cols = k_ref.shape[0]
    auxes = [part[cols:, :].astype(F32) for part in parts]
    done = []
    for head in range(cols // HD):
        at = slice(head * HD, (head + 1) * HD)
        q, k = q_ref[at, :].astype(F32), k_ref[at, :].astype(F32)
        own = jnp.sum(q * k, axis=0, keepdims=True) + rows_ref[8 * head : 8 * head + 1, :]
        lses = [sum(aux[3 * head + i : 3 * head + i + 1, :] for i in range(3)) for aux in auxes]
        top = own
        for lse in lses:
            top = jnp.maximum(top, lse)
        weight = jnp.exp(own - top)
        whole = weight
        acc = weight * v_ref[at, :].astype(F32)
        for lse, part in zip(lses, parts):
            weight = jnp.exp(lse - top)
            whole = whole + weight
            acc = acc + weight * part[at, :].astype(F32)
        done.append(acc / whole)
    attn_ref[...] = jnp.concatenate(done, axis=0).T.astype(BF16)


def project_kernel(tok_ref, *refs):
    out_ref = refs[-1]
    half = (len(refs) - 1) // 2
    acc = None
    for attn, w in zip(refs[:half], refs[half : 2 * half]):
        term = jnp.dot(attn[...], w[...], preferred_element_type=F32)
        acc = term if acc is None else acc + term
    out_ref[...] = (tok_ref[...].astype(F32) + acc).astype(BF16)


def xor(axis, k):
    return [(i, i ^ k) for i in range(lax.axis_size(axis))]


def dense_body(
    tokens,
    norm_gain,
    w_qkv,
    w_out,
    head_bias,
    kv_pool,
    key_variate,
    page_table,
    node_len,
    path_nodes,
    query_variate,
):
    rows, width = tokens.shape
    cols = w_qkv.shape[2]
    heads = cols // HD
    pages, page = key_variate.shape
    slots = pages * page
    groups = [2 * k for k in range(max(1, lax.axis_size("seq") // 2))]

    pool = kv_pool.reshape(slots, 2, cols)
    pool2 = lax.ppermute(pool, "seq", xor("seq", 1))

    w3 = w_qkv.transpose(1, 0, 2)
    smem = lambda *dims: pltpu.SMEM(dims, I32)
    msg, normed, bias, code, tok = call(
        query_kernel,
        [
            shape(cols + AUX, rows),
            shape(rows, width),
            shape(8 * heads, rows, dtype=F32),
            shape(pages, page, dtype=I32),
            shape(rows, width),
        ],
        tokens, norm_gain[None], w3, query_variate[None], path_nodes.T, head_bias, key_variate, page_table, node_len,
        flops=2 * rows * width * cols,
        away=range(8),
        scratch=[
            pltpu.VMEM((1, width), F32), pltpu.VMEM((width, cols), BF16), pltpu.VMEM((1, rows), I32), pltpu.VMEM((3, rows), I32),
            pltpu.VMEM((2, heads), F32), pltpu.VMEM((pages, page), I32), smem(1, pages), pltpu.SemaphoreType.DMA((8,)),
        ],
    )
    code2 = lax.ppermute(code, "seq", xor("seq", 1))
    msgs = [msg] + [lax.ppermute(msg, "seq", xor("seq", k)) for k in groups[1:]]

    w_far = lax.ppermute(w_out, "tp", xor("tp", 2))

    work = 4 * len(groups) * rows * slots * cols
    wide_rows = len(groups) * rows
    o1, lse1 = call(
        first_kernel,
        [shape(cols, wide_rows), shape(heads, wide_rows, dtype=F32)],
        bias, pool, code, *msgs,
        flops=work,
    )
    pool2, w_far = lax.optimization_barrier((pool2, w_far))
    merged = call(
        second_kernel, [shape(cols + AUX, rows)] * len(groups), bias, pool2, code2, o1, lse1, *msgs, flops=work
    )
    first, normed = lax.optimization_barrier((merged[0], normed))
    key, value = call(own_kernel, [shape(cols, rows)] * 2, normed, w3, flops=4 * rows * width * cols)
    back = [first] + [lax.ppermute(m, "seq", xor("seq", k)) for m, k in zip(merged[1:], groups[1:])]
    w_own, w_far, *back = lax.optimization_barrier((w_out, w_far, *back))
    outs = [w_own, w_far] + [lax.ppermute(w, "tp", xor("tp", 1)) for w in (w_own, w_far)]
    attn = call(combine_kernel, shape(rows, cols), bias, msg, key, value, *back)
    attns = [attn] + [lax.ppermute(attn, "tp", xor("tp", k)) for k in (2, 1, 3)]
    return call(project_kernel, shape(rows, width), tok, *attns, *outs, flops=2 * rows * width * width)


def solution(mesh):
    in_specs = (
        P("seq", None),
        P(),
        P(None, None, "tp"),
        P("tp", None),
        P(None, "tp"),
        P("seq", None, None, "tp"),
        P("seq", None),
        P("seq", None),
        P("seq"),
        P("seq", None),
        P("seq"),
    )
    out_specs = P("seq", None)
    owners, parts = mesh.shape["seq"], mesh.shape["tp"]
    dense = owners <= 8 and owners & (owners - 1) == 0 and parts == 4
    body = dense_body if dense else routed_body
    return jax.shard_map(body, mesh=mesh, in_specs=in_specs, out_specs=out_specs, check_vma=False)
```

```python
import functools

import jax
import jax.numpy as jnp
from jax import lax
from jax.experimental import pallas as pl
from jax.experimental.pallas import tpu as pltpu
from jax.sharding import PartitionSpec as P

HD = 64


def head_attend(qh, kh, vh, same, bias_same, bias_diff, valid):
    scores = jnp.dot(qh, kh.T, preferred_element_type=jnp.float32) * HD ** (-0.5)
    scores = scores + jnp.where(same, bias_same, bias_diff)
    scores = jnp.where(valid[None, :], scores, -1e30)
    peak = jnp.max(scores, axis=1)
    weights = jnp.exp(scores - peak[:, None])
    total = jnp.sum(weights, axis=1)
    mixed = (
        jnp.dot(weights.astype(jnp.bfloat16), vh, preferred_element_type=jnp.float32)
        / total[:, None]
    )
    mixed = lax.optimization_barrier(mixed.astype(jnp.bfloat16))
    return (mixed, peak, total)


def place_rows(dest, values, variates, owners, slots):
    onehot = (dest[:, None] == jnp.arange(owners, dtype=jnp.int32)[None, :]).astype(jnp.int32)
    before = jnp.cumsum(onehot, axis=0) - onehot
    slot = jnp.sum(before * onehot, axis=1)
    flat = dest * slots + slot
    width = values.shape[1]
    qbuf = (
        jnp.zeros((owners * slots, width), jnp.bfloat16)
        .at[flat]
        .set(values)
        .reshape(owners, slots, width)
    )
    vbuf = jnp.zeros((owners * slots,), jnp.int32).at[flat].set(variates).reshape(owners, slots)
    return (qbuf, vbuf, flat)


def routed_body(
    tokens,
    norm_gain,
    w_qkv,
    w_out,
    head_bias,
    kv_pool,
    key_variate,
    page_table,
    node_len,
    path_nodes,
    query_variate,
):
    tok_rows, width = tokens.shape
    heads_here = w_qkv.shape[2] // HD
    owners = lax.axis_size("seq")
    slots = min(tok_rows, 8 * tok_rows // owners)
    xf = tokens.astype(jnp.float32)
    normed = (xf * lax.rsqrt(jnp.mean(xf * xf, axis=1, keepdims=True) + 1e-05) * norm_gain).astype(
        jnp.bfloat16
    )
    qkv = jnp.dot(
        normed, w_qkv.reshape(width, 3 * heads_here * HD), preferred_element_type=jnp.float32
    ).astype(jnp.bfloat16)
    qkv = qkv.reshape(tok_rows, 3, heads_here, HD)
    query, key, value = (qkv[:, 0], qkv[:, 1], qkv[:, 2])
    order = page_table[0]
    node_slots = kv_pool.shape[0] * kv_pool.shape[1]
    pages = kv_pool[order].reshape(node_slots, 2, heads_here, HD)
    node_keys = jnp.moveaxis(pages[:, 0], 1, 0)
    node_values = jnp.moveaxis(pages[:, 1], 1, 0)
    key_var = key_variate[order].reshape(node_slots)
    valid = jnp.arange(node_slots, dtype=jnp.int32) < node_len[0]
    qflat = query.reshape(tok_rows, heads_here * HD)
    out_list, peak_list, total_list = ([], [], [])
    for level in range(3):
        qbuf, vbuf, flat = place_rows(path_nodes[:, level], qflat, query_variate, owners, slots)
        owner_qbuf = lax.all_to_all(qbuf, "seq", split_axis=0, concat_axis=0, tiled=True)
        owner_vbuf = lax.all_to_all(vbuf, "seq", split_axis=0, concat_axis=0, tiled=True)
        sources, count, cols = owner_qbuf.shape
        rows = sources * count
        heads_q = jnp.moveaxis(owner_qbuf.reshape(rows, heads_here, HD), 1, 0)
        same = owner_vbuf.reshape(rows)[:, None] == key_var[None, :]

        def per_head(xs):
            return head_attend(xs[0], xs[1], xs[2], same, xs[3], xs[4], valid)

        mixed, peak, total = lax.map(
            per_head, (heads_q, node_keys, node_values, head_bias[1], head_bias[0])
        )
        mixed = jnp.moveaxis(mixed, 0, 1).reshape(sources, count, cols)
        peak = peak.T.reshape(sources, count, heads_here)
        total = total.T.reshape(sources, count, heads_here)
        mixed_back = lax.all_to_all(mixed, "seq", split_axis=0, concat_axis=0, tiled=True)
        peak_back = lax.all_to_all(peak, "seq", split_axis=0, concat_axis=0, tiled=True)
        total_back = lax.all_to_all(total, "seq", split_axis=0, concat_axis=0, tiled=True)
        mixed = mixed_back
        peak = peak_back
        total = total_back
        out_list.append(mixed.reshape(owners * slots, -1)[flat].reshape(tok_rows, heads_here, HD))
        peak_list.append(peak.reshape(owners * slots, heads_here)[flat])
        total_list.append(total.reshape(owners * slots, heads_here)[flat])
    outs = jnp.stack(out_list, axis=1)
    peaks = jnp.stack(peak_list, axis=1)
    totals = jnp.stack(total_list, axis=1)
    own_peak = (
        jnp.sum(query.astype(jnp.float32) * key.astype(jnp.float32), axis=2) * HD ** (-0.5)
        + head_bias[1][None, :]
    )
    all_o = jnp.concatenate([value.astype(jnp.float32)[:, None], outs.astype(jnp.float32)], axis=1)
    all_m = jnp.concatenate([own_peak[:, None], peaks], axis=1)
    all_l = jnp.concatenate([jnp.ones((tok_rows, 1, heads_here), jnp.float32), totals], axis=1)
    top = jnp.max(all_m, axis=1, keepdims=True)
    scale = all_l * jnp.exp(all_m - top)
    attn = (jnp.sum(scale[..., None] * all_o, axis=1) / jnp.sum(scale, axis=1)[..., None]).astype(
        jnp.bfloat16
    )
    partial_sum = jnp.dot(
        attn.reshape(tok_rows, heads_here * HD), w_out, preferred_element_type=jnp.float32
    )
    total_sum = lax.psum(partial_sum, "tp")
    return (xf + total_sum).astype(jnp.bfloat16)


BF16, F32, I32 = jnp.bfloat16, jnp.float32, jnp.int32
AUX = 16
FAR = -1e30
VMEM = pl.BlockSpec(memory_space=pltpu.VMEM)
HBM = pl.BlockSpec(memory_space=pltpu.HBM)
SMEM = pl.BlockSpec(memory_space=pltpu.SMEM)


def call(kernel, outs, *args, flops=1, away=(), scratch=(), grant=16):
    single = not isinstance(outs, (tuple, list))
    args = [pltpu.with_memory_space_constraint(a, pltpu.HBM) if i in away else a for i, a in enumerate(args)]
    return pl.pallas_call(
        kernel,
        out_shape=outs,
        scratch_shapes=scratch,
        in_specs=[HBM if i in away else SMEM if a.size == 1 else VMEM for i, a in enumerate(args)],
        out_specs=VMEM if single else [VMEM] * len(outs),
        compiler_params=pltpu.CompilerParams(vmem_limit_bytes=grant << 20),
        cost_estimate=pl.CostEstimate(flops=1, bytes_accessed=1, transcendentals=0),
    )(*args)


def shape(*dims, dtype=BF16):
    return jax.ShapeDtypeStruct(dims, dtype)


def fetch(sems, *pairs):
    copies = [pltpu.make_async_copy(src, dst, sems.at[i]) for i, (src, dst) in enumerate(pairs)]
    for copy in copies:
        copy.start()
    return copies


def code_kernel(len_ref, slot_hbm, table_hbm, code_ref, slot_ref, table_ref, sems):
    for copy in fetch(sems, (slot_hbm, slot_ref), (table_hbm, table_ref)):
        copy.wait()
    pages, page = slot_ref.shape
    length = len_ref[0]
    offset = lax.broadcasted_iota(I32, (1, page), 1)
    for p in range(pages):
        place = sum(jnp.where(table_ref[0, i] == p, i, 0) for i in range(pages))
        code_ref[p : p + 1, :] = jnp.where(place * page + offset < length, slot_ref[p : p + 1, :], 8)


def query_kernel(
    tok_hbm, gain_hbm, w_hbm, variate_hbm, path_hbm, bias_hbm, pool_hbm,
    msg_ref, normed_ref, rows_ref, tok_ref, pool_ref,
    gain_ref, w_ref, variate_ref, path_ref, bias_ref, sems,
):
    copies = fetch(
        sems, (tok_hbm, tok_ref), (w_hbm.at[0], w_ref), (gain_hbm, gain_ref), (variate_hbm, variate_ref), (path_hbm, path_ref),
        (bias_hbm, bias_ref), (pool_hbm, pool_ref),
    )
    for copy in copies[2:6]:
        copy.wait()
    rows, cols = tok_ref.shape[0], w_ref.shape[1]
    for head in range(cols // HD):
        same = jnp.full((1, rows), bias_ref[1, head], F32)
        other = jnp.full((1, rows), bias_ref[0, head], F32)
        rows_ref[8 * head : 8 * head + 8, :] = jnp.concatenate([same, other, same - other, jnp.zeros((5, rows), F32)], axis=0)
    aux = [variate_ref[...].astype(F32), path_ref[...].astype(F32), jnp.zeros((AUX - 4, rows), F32)]
    msg_ref[cols:, :] = jnp.concatenate(aux, axis=0).astype(BF16)
    copies[0].wait()
    x = tok_ref[...].astype(F32)
    r = lax.rsqrt(jnp.mean(x * x, axis=1, keepdims=True) + 1e-05)
    normed = (x * r * gain_ref[...]).astype(BF16)
    normed_ref[...] = normed
    copies[1].wait()
    q = jnp.dot(normed, w_ref[...], preferred_element_type=F32).astype(BF16)
    msg_ref[:cols, :] = (q.astype(F32) * HD ** (-0.5)).T.astype(BF16)
    copies[6].wait()


def split3(x):
    a = x.astype(BF16).astype(F32)
    b = (x - a).astype(BF16).astype(F32)
    return a, b, (x - a - b).astype(BF16).astype(F32)


def split_pool(*pool_refs):
    cols = pool_refs[0].shape[2]
    i = lax.broadcasted_iota(I32, (256, 256), 0)
    j = lax.broadcasted_iota(I32, (256, 256), 1)
    pick = jnp.where(j == 2 * (i % 128) + i // 128, 1.0, 0.0).astype(BF16)
    keys, values = [], []
    for both in [ref[at : at + 128].reshape(256, cols) for ref in pool_refs for at in range(0, ref.shape[0], 128)]:
        apart = jnp.dot(pick, both, preferred_element_type=F32)
        keys.append(apart[:128].astype(BF16))
        values.append(apart[128:].T.astype(BF16))
    return jnp.concatenate(keys, axis=0), jnp.concatenate(values, axis=1)


def slot_terms(code_ref):
    pages, page = code_ref.shape
    sub = lax.broadcasted_iota(I32, (128, page), 0)
    blocks = []
    for p in range(pages):
        code = jnp.broadcast_to(code_ref[p : p + 1, :], (128, page))
        hit = ((code == sub % 8) & (sub < 24)) | ((sub >= 24) & (sub < 27))
        term = jnp.where(hit, 1.0, 0.0)
        term = jnp.where((sub == 27) & (code == 8), FAR, term)
        blocks.append(term.T.astype(BF16))
    return jnp.concatenate(blocks, axis=0)


def row_terms(bias, variate):
    rows = variate.shape[1]
    sub = lax.broadcasted_iota(I32, (8, rows), 0)
    hit = variate == sub
    other, step = split3(bias[1:2, :]), split3(bias[2:3, :])
    picked = [jnp.where(hit, jnp.broadcast_to(piece, (8, rows)), 0.0) for piece in step]
    tail = jnp.where(sub == 3, 1.0, 0.0)
    for at, piece in enumerate(other):
        tail = jnp.where(sub == at, piece, tail)
    top = jnp.concatenate(picked + [tail], axis=0).astype(BF16)
    return jnp.concatenate([top, jnp.zeros((96, rows), BF16)], axis=0)


def attend(q, keys, values_t, terms, bias, variate, head):
    pair = head // 2
    q_head = q[head * HD : (head + 1) * HD, :]
    zero = jnp.zeros_like(q_head)
    both = [q_head, zero] if head % 2 == 0 else [zero, q_head]
    q_cat = jnp.concatenate(both + [row_terms(bias, variate)], axis=0)
    k_cat = jnp.concatenate([keys[:, pair * 128 : (pair + 1) * 128], terms], axis=1)
    scores = jnp.dot(k_cat, q_cat, preferred_element_type=F32)
    peak = jnp.max(scores, axis=0, keepdims=True)
    weights = jnp.exp(scores - peak)
    total = jnp.sum(weights, axis=0, keepdims=True)
    mixed = jnp.dot(values_t[head * HD : (head + 1) * HD, :], weights.astype(BF16), preferred_element_type=F32)
    return (mixed / total).astype(BF16), peak + jnp.log(total)


def wide(rows_ref, head, blocks):
    return jnp.concatenate([rows_ref[8 * head : 8 * head + 8, :]] * blocks, axis=1)


def gather_rows(msgs, cols):
    q = jnp.concatenate([msg[:cols, :] for msg in msgs], axis=1)
    aux = jnp.concatenate([msg[cols:, :].astype(F32).astype(I32) for msg in msgs], axis=1)
    return q, aux


def own_kernel(normed_ref, w_ref, pool_ref, code_ref, k_ref, v_ref, keys_ref, values_ref, terms_ref):
    for i, own_ref in ((1, k_ref), (2, v_ref)):
        own = jnp.dot(normed_ref[...], w_ref[i], preferred_element_type=F32).astype(BF16)
        own_ref[...] = own.astype(F32).T.astype(BF16)
    keys_ref[...], values_ref[...] = split_pool(pool_ref)
    terms_ref[...] = slot_terms(code_ref)


def first_kernel(rows_ref, keys_ref, values_ref, terms_ref, *refs):
    msgs, (o_ref, lse_ref) = refs[:-2], refs[-2:]
    keys, values_t, terms = keys_ref[...], values_ref[...], terms_ref[...]
    cols = keys.shape[1]
    q, aux = gather_rows(msgs, cols)
    for head in range(cols // HD):
        o, lse = attend(q, keys, values_t, terms, wide(rows_ref, head, len(msgs)), aux[0:1, :], head)
        o_ref[head * HD : (head + 1) * HD, :] = o
        lse_ref[head : head + 1, :] = lse


def second_kernel(rows_ref, pool_ref, code_ref, o_ref, lse_ref, *refs):
    count = len(refs) // 2
    msgs, outs = refs[:count], refs[count:]
    keys, values_t = split_pool(pool_ref)
    cols = keys.shape[1]
    heads = cols // HD
    rows = msgs[0].shape[1]
    terms = slot_terms(code_ref)
    q, aux = gather_rows(msgs, cols)
    me = lax.axis_index("seq")
    named = lambda node: jnp.max((aux[1:4, :] == node).astype(I32), axis=0, keepdims=True) > 0
    mine, theirs = named(me), named(me ^ 1)
    pieces = []
    for head in range(heads):
        o2, lse2 = attend(q, keys, values_t, terms, wide(rows_ref, head, count), aux[0:1, :], head)
        lse2 = jnp.where(theirs, lse2, FAR)
        lse1 = jnp.where(mine, lse_ref[head : head + 1, :], FAR)
        top = jnp.maximum(lse1, lse2)
        w1, w2 = jnp.exp(lse1 - top), jnp.exp(lse2 - top)
        o1 = o_ref[head * HD : (head + 1) * HD, :].astype(F32)
        merged = ((w1 * o1 + w2 * o2.astype(F32)) / (w1 + w2)).astype(BF16)
        for b, out in enumerate(outs):
            out[head * HD : (head + 1) * HD, :] = merged[:, b * rows : (b + 1) * rows]
        pieces += split3(top + jnp.log(w1 + w2))
    pieces.append(jnp.zeros((AUX - 3 * heads, count * rows), F32))
    tail = jnp.concatenate(pieces, axis=0).astype(BF16)
    for b, out in enumerate(outs):
        out[cols:, :] = tail[:, b * rows : (b + 1) * rows]


def combine_kernel(rows_ref, q_ref, k_ref, v_ref, *refs):
    parts, attn_ref = refs[:-1], refs[-1]
    cols = k_ref.shape[0]
    auxes = [part[cols:, :].astype(F32) for part in parts]
    done = []
    for head in range(cols // HD):
        at = slice(head * HD, (head + 1) * HD)
        q, k = q_ref[at, :].astype(F32), k_ref[at, :].astype(F32)
        own = jnp.sum(q * k, axis=0, keepdims=True) + rows_ref[8 * head : 8 * head + 1, :]
        lses = [sum(aux[3 * head + i : 3 * head + i + 1, :] for i in range(3)) for aux in auxes]
        top = own
        for lse in lses:
            top = jnp.maximum(top, lse)
        weight = jnp.exp(own - top)
        whole = weight
        acc = weight * v_ref[at, :].astype(F32)
        for lse, part in zip(lses, parts):
            weight = jnp.exp(lse - top)
            whole = whole + weight
            acc = acc + weight * part[at, :].astype(F32)
        done.append(acc / whole)
    attn_ref[...] = jnp.concatenate(done, axis=0).T.astype(BF16)


def project_kernel(base_ref, *refs):
    *pairs, out_ref = refs
    half = len(pairs) // 2
    total = base_ref[...].astype(F32)
    for attn, w in zip(pairs[:half], pairs[half:]):
        total = total + jnp.dot(attn[...], w[...], preferred_element_type=F32)
    out_ref[...] = total.astype(out_ref.dtype)


def xor(axis, k):
    return [(i, i ^ k) for i in range(lax.axis_size(axis))]


def dense_body(
    tokens,
    norm_gain,
    w_qkv,
    w_out,
    head_bias,
    kv_pool,
    key_variate,
    page_table,
    node_len,
    path_nodes,
    query_variate,
):
    rows, width = tokens.shape
    cols = w_qkv.shape[2]
    heads = cols // HD
    pages, page = key_variate.shape
    slots = pages * page
    groups = [0] + [2 * k for k in reversed(range(1, lax.axis_size("seq") // 2))]

    pool = kv_pool.reshape(slots, 2, cols)
    pool2 = lax.ppermute(pool, "seq", xor("seq", 1))
    w_far = lax.ppermute(w_out, "tp", xor("tp", 2))

    w3 = w_qkv.transpose(1, 0, 2)
    msg, normed, bias, tok, pool = call(
        query_kernel,
        [
            shape(cols + AUX, rows), shape(rows, width), shape(8 * heads, rows, dtype=F32), shape(rows, width), shape(slots, 2, cols),
        ],
        tokens, norm_gain[None], w3, query_variate[None], path_nodes.T, head_bias, pool,
        away=range(7),
        scratch=[
            pltpu.VMEM((1, width), F32), pltpu.VMEM((width, cols), BF16), pltpu.VMEM((1, rows), I32), pltpu.VMEM((3, rows), I32),
            pltpu.VMEM((2, heads), F32), pltpu.SemaphoreType.DMA((7,)),
        ],
    )
    msgs = [msg] + [lax.ppermute(msg, "seq", xor("seq", k)) for k in groups[1:]]
    count = len(msgs)

    node_len, normed = lax.optimization_barrier((node_len, normed))
    code = call(
        code_kernel, shape(pages, page, dtype=I32), node_len, key_variate, page_table,
        away=(1, 2),
        scratch=[pltpu.VMEM((pages, page), I32), pltpu.SMEM((1, pages), I32), pltpu.SemaphoreType.DMA((2,))],
    )
    code2 = lax.ppermute(code, "seq", xor("seq", 1))
    key, value, keys, values_t, terms = call(
        own_kernel,
        [shape(cols, rows), shape(cols, rows), shape(slots, cols), shape(cols, slots), shape(slots, 128)],
        normed, w3, pool, code,
    )

    wide_rows = count * rows
    o1, lse1 = call(
        first_kernel, [shape(cols, wide_rows), shape(heads, wide_rows, dtype=F32)], bias, keys, values_t, terms, *msgs
    )
    pool2, w_far = lax.optimization_barrier((pool2, w_far))
    merged = call(second_kernel, [shape(cols + AUX, rows)] * count, bias, pool2, code2, o1, lse1, *msgs)
    back = [merged[0]] + [lax.ppermute(m, "seq", xor("seq", k)) for m, k in zip(merged[1:], groups[1:])]
    w_own, w_far, *back = lax.optimization_barrier((w_out, w_far, *back))
    w_near, w_last = (lax.ppermute(w, "tp", xor("tp", 1)) for w in (w_own, w_far))
    attn = call(combine_kernel, shape(rows, cols), bias, msg, key, value, *back)
    x_near, x_far, x_last = (lax.ppermute(attn, "tp", xor("tp", k)) for k in (1, 2, 3))
    total = call(project_kernel, shape(rows, width, dtype=F32), tok, attn, x_near, w_own, w_near)
    return call(project_kernel, shape(rows, width), total, x_far, x_last, w_far, w_last)


def solution(mesh):
    in_specs = (
        P("seq", None),
        P(),
        P(None, None, "tp"),
        P("tp", None),
        P(None, "tp"),
        P("seq", None, None, "tp"),
        P("seq", None),
        P("seq", None),
        P("seq"),
        P("seq", None),
        P("seq"),
    )
    out_specs = P("seq", None)
    owners, parts = mesh.shape["seq"], mesh.shape["tp"]
    dense = owners <= 8 and owners & (owners - 1) == 0 and parts == 4
    body = dense_body if dense else routed_body
    return jax.shard_map(body, mesh=mesh, in_specs=in_specs, out_specs=out_specs, check_vma=False)
```

```python
import jax
import jax.numpy as jnp
from jax import lax
from jax.experimental import pallas as pl
from jax.experimental.pallas import tpu as pltpu
from jax.sharding import PartitionSpec as P

HD = 64


def head_attend(qh, kh, vh, same, bias_same, bias_diff, valid):
    scores = jnp.dot(qh, kh.T, preferred_element_type=jnp.float32) * HD ** (-0.5)
    scores = scores + jnp.where(same, bias_same, bias_diff)
    scores = jnp.where(valid[None, :], scores, -1e30)
    peak = jnp.max(scores, axis=1)
    weights = jnp.exp(scores - peak[:, None])
    total = jnp.sum(weights, axis=1)
    mixed = (
        jnp.dot(weights.astype(jnp.bfloat16), vh, preferred_element_type=jnp.float32)
        / total[:, None]
    )
    mixed = lax.optimization_barrier(mixed.astype(jnp.bfloat16))
    return (mixed, peak, total)


def place_rows(dest, values, variates, owners, slots):
    onehot = (dest[:, None] == jnp.arange(owners, dtype=jnp.int32)[None, :]).astype(jnp.int32)
    before = jnp.cumsum(onehot, axis=0) - onehot
    slot = jnp.sum(before * onehot, axis=1)
    flat = dest * slots + slot
    width = values.shape[1]
    qbuf = (
        jnp.zeros((owners * slots, width), jnp.bfloat16)
        .at[flat]
        .set(values)
        .reshape(owners, slots, width)
    )
    vbuf = jnp.zeros((owners * slots,), jnp.int32).at[flat].set(variates).reshape(owners, slots)
    return (qbuf, vbuf, flat)


def routed_body(
    tokens,
    norm_gain,
    w_qkv,
    w_out,
    head_bias,
    kv_pool,
    key_variate,
    page_table,
    node_len,
    path_nodes,
    query_variate,
):
    tok_rows, width = tokens.shape
    heads_here = w_qkv.shape[2] // HD
    owners = lax.axis_size("seq")
    slots = min(tok_rows, 8 * tok_rows // owners)
    xf = tokens.astype(jnp.float32)
    normed = (xf * lax.rsqrt(jnp.mean(xf * xf, axis=1, keepdims=True) + 1e-05) * norm_gain).astype(
        jnp.bfloat16
    )
    qkv = jnp.dot(
        normed, w_qkv.reshape(width, 3 * heads_here * HD), preferred_element_type=jnp.float32
    ).astype(jnp.bfloat16)
    qkv = qkv.reshape(tok_rows, 3, heads_here, HD)
    query, key, value = (qkv[:, 0], qkv[:, 1], qkv[:, 2])
    order = page_table[0]
    node_slots = kv_pool.shape[0] * kv_pool.shape[1]
    pages = kv_pool[order].reshape(node_slots, 2, heads_here, HD)
    node_keys = jnp.moveaxis(pages[:, 0], 1, 0)
    node_values = jnp.moveaxis(pages[:, 1], 1, 0)
    key_var = key_variate[order].reshape(node_slots)
    valid = jnp.arange(node_slots, dtype=jnp.int32) < node_len[0]
    qflat = query.reshape(tok_rows, heads_here * HD)
    out_list, peak_list, total_list = ([], [], [])
    for level in range(3):
        qbuf, vbuf, flat = place_rows(path_nodes[:, level], qflat, query_variate, owners, slots)
        owner_qbuf = lax.all_to_all(qbuf, "seq", split_axis=0, concat_axis=0, tiled=True)
        owner_vbuf = lax.all_to_all(vbuf, "seq", split_axis=0, concat_axis=0, tiled=True)
        sources, count, cols = owner_qbuf.shape
        rows = sources * count
        heads_q = jnp.moveaxis(owner_qbuf.reshape(rows, heads_here, HD), 1, 0)
        same = owner_vbuf.reshape(rows)[:, None] == key_var[None, :]

        def per_head(xs):
            return head_attend(xs[0], xs[1], xs[2], same, xs[3], xs[4], valid)

        mixed, peak, total = lax.map(
            per_head, (heads_q, node_keys, node_values, head_bias[1], head_bias[0])
        )
        mixed = jnp.moveaxis(mixed, 0, 1).reshape(sources, count, cols)
        peak = peak.T.reshape(sources, count, heads_here)
        total = total.T.reshape(sources, count, heads_here)
        mixed_back = lax.all_to_all(mixed, "seq", split_axis=0, concat_axis=0, tiled=True)
        peak_back = lax.all_to_all(peak, "seq", split_axis=0, concat_axis=0, tiled=True)
        total_back = lax.all_to_all(total, "seq", split_axis=0, concat_axis=0, tiled=True)
        mixed = mixed_back
        peak = peak_back
        total = total_back
        out_list.append(mixed.reshape(owners * slots, -1)[flat].reshape(tok_rows, heads_here, HD))
        peak_list.append(peak.reshape(owners * slots, heads_here)[flat])
        total_list.append(total.reshape(owners * slots, heads_here)[flat])
    outs = jnp.stack(out_list, axis=1)
    peaks = jnp.stack(peak_list, axis=1)
    totals = jnp.stack(total_list, axis=1)
    own_peak = (
        jnp.sum(query.astype(jnp.float32) * key.astype(jnp.float32), axis=2) * HD ** (-0.5)
        + head_bias[1][None, :]
    )
    all_o = jnp.concatenate([value.astype(jnp.float32)[:, None], outs.astype(jnp.float32)], axis=1)
    all_m = jnp.concatenate([own_peak[:, None], peaks], axis=1)
    all_l = jnp.concatenate([jnp.ones((tok_rows, 1, heads_here), jnp.float32), totals], axis=1)
    top = jnp.max(all_m, axis=1, keepdims=True)
    scale = all_l * jnp.exp(all_m - top)
    attn = (jnp.sum(scale[..., None] * all_o, axis=1) / jnp.sum(scale, axis=1)[..., None]).astype(
        jnp.bfloat16
    )
    partial_sum = jnp.dot(
        attn.reshape(tok_rows, heads_here * HD), w_out, preferred_element_type=jnp.float32
    )
    total_sum = lax.psum(partial_sum, "tp")
    return (xf + total_sum).astype(jnp.bfloat16)


BF16, F32, I32 = jnp.bfloat16, jnp.float32, jnp.int32
AUX = 16
FAR = -1e30
PAGE = 128
MATES = (1, 2)
PEERS = ((6, 5), (4, 4), (2, 1))
VMEM = pl.BlockSpec(memory_space=pltpu.VMEM)
HBM = pl.BlockSpec(memory_space=pltpu.HBM)
SMEM = pl.BlockSpec(memory_space=pltpu.SMEM)


def call(kernel, outs, *args, flops=1, away=(), scratch=(), leaves=False):
    single = not isinstance(outs, (tuple, list))
    args = [pltpu.with_memory_space_constraint(a, pltpu.HBM) if i in away else a for i, a in enumerate(args)]
    return pl.pallas_call(
        kernel,
        out_shape=outs,
        scratch_shapes=scratch,
        in_specs=[HBM if i in away else SMEM if a.size == 1 else VMEM for i, a in enumerate(args)],
        out_specs=HBM if leaves else VMEM if single else [VMEM] * len(outs),
        compiler_params=pltpu.CompilerParams(vmem_limit_bytes=16 << 20),
        cost_estimate=pl.CostEstimate(flops=flops, bytes_accessed=1, transcendentals=0),
    )(*args)


def shape(*dims, dtype=BF16):
    return jax.ShapeDtypeStruct(dims, dtype)


def fetch(sems, *pairs):
    copies = [pltpu.make_async_copy(src, dst, sems.at[i]) for i, (src, dst) in enumerate(pairs)]
    for copy in copies:
        copy.start()
    return copies


def query_kernel(
    len_ref, tok_hbm, gain_hbm, w_hbm, variate_hbm, path_hbm, bias_hbm, slot_hbm, table_hbm, pool_hbm,
    msg_ref, normed_ref, rows_ref, tok_ref, pool_ref,
    gain_ref, w_ref, variate_ref, path_ref, bias_ref, slot_ref, table_ref, sems,
):
    pages, page = slot_ref.shape
    slots = pages * page
    copies = fetch(
        sems, (tok_hbm, tok_ref), (w_hbm.at[0], w_ref), (gain_hbm, gain_ref), (variate_hbm, variate_ref), (path_hbm, path_ref),
        (bias_hbm, bias_ref), (slot_hbm, slot_ref), (table_hbm, table_ref), (pool_hbm, pool_ref.at[pl.ds(0, slots)]),
    )
    for copy in copies[2:8]:
        copy.wait()
    rows, cols = tok_ref.shape[0], w_ref.shape[1]
    length = len_ref[0]
    offset = lax.broadcasted_iota(I32, (1, page), 1)
    for p in range(pages):
        place = sum(jnp.where(table_ref[0, i] == p, i, 0) for i in range(pages))
        code = jnp.where(place * page + offset < length, slot_ref[p : p + 1, :], 8).astype(F32)
        wide_code = jnp.concatenate([code, jnp.zeros((1, cols - page), F32)], axis=1) if cols > page else code
        pool_ref[slots + p] = jnp.concatenate([wide_code, wide_code], axis=0).astype(BF16)
    for head in range(cols // HD):
        same = jnp.full((1, rows), bias_ref[1, head], F32)
        other = jnp.full((1, rows), bias_ref[0, head], F32)
        rows_ref[8 * head : 8 * head + 8, :] = jnp.concatenate([same, other, same - other, jnp.zeros((5, rows), F32)], axis=0)
    aux = [variate_ref[...].astype(F32), path_ref[...].astype(F32), jnp.zeros((AUX - 4, rows), F32)]
    msg_ref[cols:, :] = jnp.concatenate(aux, axis=0).astype(BF16)
    copies[0].wait()
    x = tok_ref[...].astype(F32)
    r = lax.rsqrt(jnp.mean(x * x, axis=1, keepdims=True) + 1e-05)
    normed = (x * r * gain_ref[...]).astype(BF16)
    normed_ref[...] = normed
    copies[1].wait()
    q = jnp.dot(normed, w_ref[...], preferred_element_type=F32).astype(BF16)
    msg_ref[:cols, :] = (q.astype(F32) * HD ** (-0.5)).T.astype(BF16)
    copies[8].wait()


def split3(x):
    a = x.astype(BF16).astype(F32)
    b = (x - a).astype(BF16).astype(F32)
    return a, b, (x - a - b).astype(BF16).astype(F32)


def split_pool(pool_ref):
    rows, _, cols = pool_ref.shape
    pages = rows // (PAGE + 1)
    i = lax.broadcasted_iota(I32, (2 * PAGE, 2 * PAGE), 0)
    j = lax.broadcasted_iota(I32, (2 * PAGE, 2 * PAGE), 1)
    pick = jnp.where(j == 2 * (i % PAGE) + i // PAGE, 1.0, 0.0).astype(BF16)
    keys, values = [], []
    for p in range(pages):
        both = pool_ref[p * PAGE : (p + 1) * PAGE].reshape(2 * PAGE, cols)
        apart = jnp.dot(pick, both, preferred_element_type=F32)
        keys.append(apart[:PAGE].astype(BF16))
        values.append(apart[PAGE:].T.astype(BF16))
    codes = [pool_ref[pages * PAGE + p].astype(F32)[0:1, :PAGE].astype(I32) for p in range(pages)]
    return jnp.concatenate(keys, axis=0), jnp.concatenate(values, axis=1), slot_terms(codes)


def slot_terms(codes):
    sub = lax.broadcasted_iota(I32, (128, PAGE), 0)
    blocks = []
    for row in codes:
        code = jnp.broadcast_to(row, (128, PAGE))
        hit = ((code == sub % 8) & (sub < 24)) | ((sub >= 24) & (sub < 27))
        term = jnp.where(hit, 1.0, 0.0)
        term = jnp.where((sub == 27) & (code == 8), FAR, term)
        blocks.append(term.T.astype(BF16))
    return jnp.concatenate(blocks, axis=0)


def row_terms(bias, variate):
    rows = variate.shape[1]
    sub = lax.broadcasted_iota(I32, (8, rows), 0)
    hit = variate == sub
    other, step = split3(bias[1:2, :]), split3(bias[2:3, :])
    picked = [jnp.where(hit, jnp.broadcast_to(piece, (8, rows)), 0.0) for piece in step]
    tail = jnp.where(sub == 3, 1.0, 0.0)
    for at, piece in enumerate(other):
        tail = jnp.where(sub == at, piece, tail)
    top = jnp.concatenate(picked + [tail], axis=0).astype(BF16)
    return jnp.concatenate([top, jnp.zeros((96, rows), BF16)], axis=0)


def query_terms(q, rows_ref, variate):
    blocks = variate.shape[1] // rows_ref.shape[1]
    cats = []
    for head in range(q.shape[0] // HD):
        q_head = q[head * HD : (head + 1) * HD, :]
        zero = jnp.zeros_like(q_head)
        both = [q_head, zero] if head % 2 == 0 else [zero, q_head]
        cats.append(jnp.concatenate(both + [row_terms(wide(rows_ref, head, blocks), variate)], axis=0))
    return cats


def attend(cats, node):
    keys, values_t, terms = node
    scores = []
    for head, cat in enumerate(cats):
        pair = head // 2
        k_cat = jnp.concatenate([keys[:, pair * 128 : (pair + 1) * 128], terms], axis=1)
        scores.append(jnp.dot(k_cat, cat, preferred_element_type=F32))
    done = []
    for head, score in enumerate(scores):
        peak = jnp.max(score, axis=0, keepdims=True)
        weights = jnp.exp(score - peak)
        total = jnp.sum(weights, axis=0, keepdims=True)
        mixed = jnp.dot(values_t[head * HD : (head + 1) * HD, :], weights.astype(BF16), preferred_element_type=F32)
        done.append(((mixed / total).astype(BF16), peak + jnp.log(total)))
    return done


def wide(rows_ref, head, blocks):
    return jnp.concatenate([rows_ref[8 * head : 8 * head + 8, :]] * blocks, axis=1)


def gather_rows(msgs, cols):
    q = jnp.concatenate([msg[:cols, :] for msg in msgs], axis=1)
    aux = jnp.concatenate([msg[cols:, :].astype(F32).astype(I32) for msg in msgs], axis=1)
    return q, aux


def own_kernel(normed_ref, w_ref, pool_ref, out_hbm, k_ref, v_ref, keys_ref, values_ref, terms_ref, out_ref, sem):
    copy = pltpu.make_async_copy(out_hbm, out_ref, sem)
    copy.start()
    for i, own_ref in ((1, k_ref), (2, v_ref)):
        own = jnp.dot(normed_ref[...], w_ref[i], preferred_element_type=F32).astype(BF16)
        own_ref[...] = own.astype(F32).T.astype(BF16)
    keys_ref[...], values_ref[...], terms_ref[...] = split_pool(pool_ref)
    copy.wait()


def pair_terms(rows_ref, mine, theirs, msgs, outs):
    count = len(msgs)
    cols = mine[0].shape[1]
    rows = msgs[0].shape[1]
    q, aux = gather_rows(msgs, cols)
    cats = query_terms(q, rows_ref, aux[0:1, :])
    me = lax.axis_index("seq")
    mate = me ^ jnp.where(lax.axis_index("tp") % 2 == 0, MATES[0], MATES[1])
    named = lambda node: jnp.max((aux[1:4, :] == node).astype(I32), axis=0, keepdims=True) > 0
    named_1, named_2 = named(me), named(mate)
    pieces = []
    for head, ((o1, lse1), (o2, lse2)) in enumerate(zip(attend(cats, mine), attend(cats, theirs))):
        lse1 = jnp.where(named_1, lse1, FAR)
        lse2 = jnp.where(named_2, lse2, FAR)
        top = jnp.maximum(lse1, lse2)
        w1, w2 = jnp.exp(lse1 - top), jnp.exp(lse2 - top)
        merged = ((w1 * o1.astype(F32) + w2 * o2.astype(F32)) / (w1 + w2)).astype(BF16)
        for b, out in enumerate(outs):
            out[head * HD : (head + 1) * HD, :] = merged[:, b * rows : (b + 1) * rows]
        pieces += split3(top + jnp.log(w1 + w2))
    pieces.append(jnp.zeros((AUX - len(pieces), count * rows), F32))
    tail = jnp.concatenate(pieces, axis=0).astype(BF16)
    for b, out in enumerate(outs):
        out[cols:, :] = tail[:, b * rows : (b + 1) * rows]


def far_kernel(rows_ref, keys_ref, values_ref, terms_ref, pool_ref, *refs):
    count = (len(refs) - 3) // 2
    mate = split_pool(pool_ref)
    pair_terms(rows_ref, (keys_ref[...], values_ref[...], terms_ref[...]), mate, refs[:count], refs[count : 2 * count])
    for ref, value in zip(refs[2 * count :], mate):
        ref[...] = value


def near_kernel(rows_ref, *refs):
    nodes, refs = [ref[...] for ref in refs[:6]], refs[6:]
    count = len(refs) // 2
    pair_terms(rows_ref, nodes[:3], nodes[3:], refs[:count], refs[count:])


def add_parts(acc, parts, cols):
    auxes = [part[cols:, :].astype(F32) for part in parts]
    for head, (top, whole, total) in enumerate(acc):
        at = slice(head * HD, (head + 1) * HD)
        lses = [sum(aux[3 * head + i : 3 * head + i + 1, :] for i in range(3)) for aux in auxes]
        peak = top
        for lse in lses:
            peak = jnp.maximum(peak, lse)
        weight = jnp.exp(top - peak)
        whole, total = weight * whole, weight * total
        for lse, part in zip(lses, parts):
            weight = jnp.exp(lse - peak)
            whole = whole + weight
            total = total + weight * part[at, :].astype(F32)
        yield peak, whole, total


def combine_far_kernel(rows_ref, q_ref, k_ref, v_ref, *refs):
    *parts, acc_ref, side_ref = refs
    cols = k_ref.shape[0]
    acc = []
    for head in range(cols // HD):
        at = slice(head * HD, (head + 1) * HD)
        q, k = q_ref[at, :].astype(F32), k_ref[at, :].astype(F32)
        own = jnp.sum(q * k, axis=0, keepdims=True) + rows_ref[8 * head : 8 * head + 1, :]
        acc.append((own, jnp.ones_like(own), v_ref[at, :].astype(F32)))
    for head, (top, whole, total) in enumerate(add_parts(acc, parts, cols)):
        acc_ref[head * HD : (head + 1) * HD, :] = total
        side_ref[2 * head : 2 * head + 2, :] = jnp.concatenate([top, whole], axis=0)


def combine_near_kernel(acc_ref, side_ref, *refs):
    *parts, attn_ref = refs
    cols = acc_ref.shape[0]
    acc = [
        (side_ref[2 * head : 2 * head + 1, :], side_ref[2 * head + 1 : 2 * head + 2, :], acc_ref[head * HD : (head + 1) * HD, :])
        for head in range(cols // HD)
    ]
    done = [total / whole for _, whole, total in add_parts(acc, parts, cols)]
    attn_ref[...] = jnp.concatenate(done, axis=0).T.astype(BF16)


def project_kernel(base_ref, *refs):
    *pairs, out_ref = refs
    half = len(pairs) // 2
    total = base_ref[...].astype(F32)
    for attn, w in zip(pairs[:half], pairs[half:]):
        total = total + jnp.dot(attn[...], w[...], preferred_element_type=F32)
    out_ref[...] = total.astype(out_ref.dtype)


def last_kernel(base_ref, *refs):
    *pairs, out_hbm, out_ref, sems = refs
    half = len(pairs) // 2
    step = 256
    copies = []
    for i, at in enumerate(range(0, base_ref.shape[1], step)):
        span = slice(at, at + step)
        total = base_ref[:, span]
        for attn, w in zip(pairs[:half], pairs[half:]):
            total = total + jnp.dot(attn[...], w[:, span], preferred_element_type=F32)
        out_ref[:, span] = total.astype(out_ref.dtype)
        copies.append(pltpu.make_async_copy(out_ref.at[:, span], out_hbm.at[:, span], sems.at[i]))
        copies[-1].start()
    for copy in copies:
        copy.wait()


def swap(x, masks):
    owners, parts = lax.axis_size("seq"), lax.axis_size("tp")
    pairs = [(i * parts + t, (i ^ masks[t % 2]) * parts + t) for i in range(owners) for t in range(parts)]
    return lax.ppermute(x, ("seq", "tp"), pairs)


def across(x, mask):
    return lax.ppermute(x, "tp", [(t, t ^ mask) for t in range(lax.axis_size("tp"))])


def dense_body(
    tokens,
    norm_gain,
    w_qkv,
    w_out,
    head_bias,
    kv_pool,
    key_variate,
    page_table,
    node_len,
    path_nodes,
    query_variate,
):
    rows, width = tokens.shape
    cols = w_qkv.shape[2]
    heads = cols // HD
    pages, page = key_variate.shape
    slots = pages * page

    w3 = w_qkv.transpose(1, 0, 2)
    msg, normed, bias, tok, pool = call(
        query_kernel,
        [
            shape(cols + AUX, rows), shape(rows, width), shape(8 * heads, rows, dtype=F32), shape(rows, width),
            shape(slots + pages, 2, cols),
        ],
        node_len, tokens, norm_gain[None], w3, query_variate[None], path_nodes.T, head_bias, key_variate, page_table,
        kv_pool.reshape(slots, 2, cols),
        away=range(1, 10),
        scratch=[
            pltpu.VMEM((1, width), F32), pltpu.VMEM((width, cols), BF16), pltpu.VMEM((1, rows), I32), pltpu.VMEM((3, rows), I32),
            pltpu.VMEM((2, heads), F32), pltpu.VMEM((pages, page), I32), pltpu.SMEM((1, pages), I32),
            pltpu.SemaphoreType.DMA((9,)),
        ],
    )
    msgs = [msg] + [swap(msg, peer) for peer in PEERS]
    pool2 = swap(pool, MATES)

    key, value, keys, values_t, terms, w_own = call(
        own_kernel,
        [
            shape(cols, rows), shape(cols, rows), shape(slots, cols), shape(cols, slots), shape(slots, 128), shape(cols, width),
        ],
        normed, w3, pool, w_out,
        flops=115300000,
        away=(3,),
        scratch=[pltpu.SemaphoreType.DMA],
    )
    w_far = across(w_own, 2)
    far = len(PEERS) - 1
    node = [shape(slots, cols), shape(cols, slots), shape(slots, 128)]
    message = shape(cols + AUX, rows)
    *far_out, keys2, values2, terms2 = call(
        far_kernel, [message] * far + node, bias, keys, values_t, terms, pool2, *msgs[1 : 1 + far], flops=2306000000
    )
    own_out, near_out = call(
        near_kernel, [message] * 2, bias, keys, values_t, terms, keys2, values2, terms2, msgs[0], msgs[-1], flops=2306000000
    )
    far_back = [swap(m, peer) for m, peer in zip(far_out, PEERS)]
    near_back = swap(near_out, PEERS[-1])
    acc, side = call(
        combine_far_kernel, [shape(cols, rows, dtype=F32), shape(2 * heads, rows, dtype=F32)],
        bias, msg, key, value, *far_back,
        flops=4612000000,
    )
    w_own, w_far, acc, near_back = lax.optimization_barrier((w_own, w_far, acc, near_back))
    w_near, w_last = across(w_own, 1), across(w_far, 1)
    attn = call(combine_near_kernel, shape(rows, cols), acc, side, own_out, near_back, flops=115300000)
    x_near, x_far, x_last = (across(attn, k) for k in (1, 2, 3))
    total = call(project_kernel, shape(rows, width, dtype=F32), tok, attn, x_near, w_own, w_near)
    return call(
        last_kernel, shape(rows, width), total, x_far, x_last, w_far, w_last,
        scratch=[pltpu.VMEM((rows, width), BF16), pltpu.SemaphoreType.DMA((width // 256,))],
        leaves=True,
    )


def solution(mesh):
    in_specs = (
        P("seq", None),
        P(),
        P(None, None, "tp"),
        P("tp", None),
        P(None, "tp"),
        P("seq", None, None, "tp"),
        P("seq", None),
        P("seq", None),
        P("seq"),
        P("seq", None),
        P("seq"),
    )
    out_specs = P("seq", None)
    owners, parts = mesh.shape["seq"], mesh.shape["tp"]
    dense = owners == 8 and parts == 4
    body = dense_body if dense else routed_body
    return jax.shard_map(body, mesh=mesh, in_specs=in_specs, out_specs=out_specs, check_vma=False)
```

```python
import jax
import jax.numpy as jnp
from jax import lax
from jax.experimental import pallas as pl
from jax.experimental.pallas import tpu as pltpu
from jax.sharding import PartitionSpec as P

HD = 64


def head_attend(qh, kh, vh, same, bias_same, bias_diff, valid):
    scores = jnp.dot(qh, kh.T, preferred_element_type=jnp.float32) * HD ** (-0.5)
    scores = scores + jnp.where(same, bias_same, bias_diff)
    scores = jnp.where(valid[None, :], scores, -1e30)
    peak = jnp.max(scores, axis=1)
    weights = jnp.exp(scores - peak[:, None])
    total = jnp.sum(weights, axis=1)
    mixed = (
        jnp.dot(weights.astype(jnp.bfloat16), vh, preferred_element_type=jnp.float32)
        / total[:, None]
    )
    mixed = lax.optimization_barrier(mixed.astype(jnp.bfloat16))
    return (mixed, peak, total)


def place_rows(dest, values, variates, owners, slots):
    onehot = (dest[:, None] == jnp.arange(owners, dtype=jnp.int32)[None, :]).astype(jnp.int32)
    before = jnp.cumsum(onehot, axis=0) - onehot
    slot = jnp.sum(before * onehot, axis=1)
    flat = dest * slots + slot
    width = values.shape[1]
    qbuf = (
        jnp.zeros((owners * slots, width), jnp.bfloat16)
        .at[flat]
        .set(values)
        .reshape(owners, slots, width)
    )
    vbuf = jnp.zeros((owners * slots,), jnp.int32).at[flat].set(variates).reshape(owners, slots)
    return (qbuf, vbuf, flat)


def routed_body(
    tokens,
    norm_gain,
    w_qkv,
    w_out,
    head_bias,
    kv_pool,
    key_variate,
    page_table,
    node_len,
    path_nodes,
    query_variate,
):
    tok_rows, width = tokens.shape
    heads_here = w_qkv.shape[2] // HD
    owners = lax.axis_size("seq")
    slots = min(tok_rows, 8 * tok_rows // owners)
    xf = tokens.astype(jnp.float32)
    normed = (xf * lax.rsqrt(jnp.mean(xf * xf, axis=1, keepdims=True) + 1e-05) * norm_gain).astype(
        jnp.bfloat16
    )
    qkv = jnp.dot(
        normed, w_qkv.reshape(width, 3 * heads_here * HD), preferred_element_type=jnp.float32
    ).astype(jnp.bfloat16)
    qkv = qkv.reshape(tok_rows, 3, heads_here, HD)
    query, key, value = (qkv[:, 0], qkv[:, 1], qkv[:, 2])
    order = page_table[0]
    node_slots = kv_pool.shape[0] * kv_pool.shape[1]
    pages = kv_pool[order].reshape(node_slots, 2, heads_here, HD)
    node_keys = jnp.moveaxis(pages[:, 0], 1, 0)
    node_values = jnp.moveaxis(pages[:, 1], 1, 0)
    key_var = key_variate[order].reshape(node_slots)
    valid = jnp.arange(node_slots, dtype=jnp.int32) < node_len[0]
    qflat = query.reshape(tok_rows, heads_here * HD)
    out_list, peak_list, total_list = ([], [], [])
    for level in range(3):
        qbuf, vbuf, flat = place_rows(path_nodes[:, level], qflat, query_variate, owners, slots)
        owner_qbuf = lax.all_to_all(qbuf, "seq", split_axis=0, concat_axis=0, tiled=True)
        owner_vbuf = lax.all_to_all(vbuf, "seq", split_axis=0, concat_axis=0, tiled=True)
        sources, count, cols = owner_qbuf.shape
        rows = sources * count
        heads_q = jnp.moveaxis(owner_qbuf.reshape(rows, heads_here, HD), 1, 0)
        same = owner_vbuf.reshape(rows)[:, None] == key_var[None, :]

        def per_head(xs):
            return head_attend(xs[0], xs[1], xs[2], same, xs[3], xs[4], valid)

        mixed, peak, total = lax.map(
            per_head, (heads_q, node_keys, node_values, head_bias[1], head_bias[0])
        )
        mixed = jnp.moveaxis(mixed, 0, 1).reshape(sources, count, cols)
        peak = peak.T.reshape(sources, count, heads_here)
        total = total.T.reshape(sources, count, heads_here)
        mixed_back = lax.all_to_all(mixed, "seq", split_axis=0, concat_axis=0, tiled=True)
        peak_back = lax.all_to_all(peak, "seq", split_axis=0, concat_axis=0, tiled=True)
        total_back = lax.all_to_all(total, "seq", split_axis=0, concat_axis=0, tiled=True)
        mixed = mixed_back
        peak = peak_back
        total = total_back
        out_list.append(mixed.reshape(owners * slots, -1)[flat].reshape(tok_rows, heads_here, HD))
        peak_list.append(peak.reshape(owners * slots, heads_here)[flat])
        total_list.append(total.reshape(owners * slots, heads_here)[flat])
    outs = jnp.stack(out_list, axis=1)
    peaks = jnp.stack(peak_list, axis=1)
    totals = jnp.stack(total_list, axis=1)
    own_peak = (
        jnp.sum(query.astype(jnp.float32) * key.astype(jnp.float32), axis=2) * HD ** (-0.5)
        + head_bias[1][None, :]
    )
    all_o = jnp.concatenate([value.astype(jnp.float32)[:, None], outs.astype(jnp.float32)], axis=1)
    all_m = jnp.concatenate([own_peak[:, None], peaks], axis=1)
    all_l = jnp.concatenate([jnp.ones((tok_rows, 1, heads_here), jnp.float32), totals], axis=1)
    top = jnp.max(all_m, axis=1, keepdims=True)
    scale = all_l * jnp.exp(all_m - top)
    attn = (jnp.sum(scale[..., None] * all_o, axis=1) / jnp.sum(scale, axis=1)[..., None]).astype(
        jnp.bfloat16
    )
    partial_sum = jnp.dot(
        attn.reshape(tok_rows, heads_here * HD), w_out, preferred_element_type=jnp.float32
    )
    total_sum = lax.psum(partial_sum, "tp")
    return (xf + total_sum).astype(jnp.bfloat16)


BF16, F32, I32 = jnp.bfloat16, jnp.float32, jnp.int32
AUX = 16
FAR = -1e30
MATES = (1, 2)
PEERS = ((4, 5), (6, 4), (2, 1))
VMEM = pl.BlockSpec(memory_space=pltpu.VMEM)
HBM = pl.BlockSpec(memory_space=pltpu.HBM)
SMEM = pl.BlockSpec(memory_space=pltpu.SMEM)


def call(kernel, outs, *args, flops=1, away=(), scratch=(), leaves=False):
    single = not isinstance(outs, (tuple, list))
    args = [pltpu.with_memory_space_constraint(a, pltpu.HBM) if i in away else a for i, a in enumerate(args)]
    return pl.pallas_call(
        kernel,
        out_shape=outs,
        scratch_shapes=scratch,
        in_specs=[HBM if i in away else SMEM if a.size == 1 else VMEM for i, a in enumerate(args)],
        out_specs=HBM if leaves else VMEM if single else [VMEM] * len(outs),
        compiler_params=pltpu.CompilerParams(vmem_limit_bytes=16 << 20),
        cost_estimate=pl.CostEstimate(flops=flops, bytes_accessed=1, transcendentals=0),
    )(*args)


def shape(*dims, dtype=BF16):
    return jax.ShapeDtypeStruct(dims, dtype)


def fetch(sems, *pairs):
    copies = [pltpu.make_async_copy(src, dst, sems.at[i]) for i, (src, dst) in enumerate(pairs)]
    for copy in copies:
        copy.start()
    return copies


def query_kernel(
    len_ref, tok_hbm, gain_hbm, w_hbm, variate_hbm, path_hbm, bias_hbm, slot_hbm, table_hbm, pool_hbm,
    msg_ref, normed_ref, rows_ref, tok_ref, pool_ref, code_ref,
    gain_ref, w_ref, variate_ref, path_ref, bias_ref, slot_ref, table_ref, sems,
):
    pages, page = slot_ref.shape
    copies = fetch(
        sems, (tok_hbm, tok_ref), (w_hbm.at[0], w_ref), (gain_hbm, gain_ref), (variate_hbm, variate_ref), (path_hbm, path_ref),
        (bias_hbm, bias_ref), (slot_hbm, slot_ref), (table_hbm, table_ref), (pool_hbm, pool_ref),
    )
    for copy in copies[2:8]:
        copy.wait()
    rows, cols = tok_ref.shape[0], w_ref.shape[1]
    length = len_ref[0]
    offset = lax.broadcasted_iota(I32, (1, page), 1)
    for p in range(pages):
        place = sum(jnp.where(table_ref[0, i] == p, i, 0) for i in range(pages))
        code_ref[p : p + 1, :] = jnp.where(place * page + offset < length, slot_ref[p : p + 1, :], 8)
    for head in range(cols // HD):
        same = jnp.full((1, rows), bias_ref[1, head], F32)
        other = jnp.full((1, rows), bias_ref[0, head], F32)
        rows_ref[8 * head : 8 * head + 8, :] = jnp.concatenate([same, other, same - other, jnp.zeros((5, rows), F32)], axis=0)
    aux = [variate_ref[...].astype(F32), path_ref[...].astype(F32), jnp.zeros((AUX - 4, rows), F32)]
    msg_ref[cols:, :] = jnp.concatenate(aux, axis=0).astype(BF16)
    copies[0].wait()
    x = tok_ref[...].astype(F32)
    r = lax.rsqrt(jnp.mean(x * x, axis=1, keepdims=True) + 1e-05)
    normed = (x * r * gain_ref[...]).astype(BF16)
    normed_ref[...] = normed
    copies[1].wait()
    q = jnp.dot(normed, w_ref[...], preferred_element_type=F32).astype(BF16)
    msg_ref[:cols, :] = (q.astype(F32) * HD ** (-0.5)).T.astype(BF16)
    copies[8].wait()


def split3(x):
    a = x.astype(BF16).astype(F32)
    b = (x - a).astype(BF16).astype(F32)
    return a, b, (x - a - b).astype(BF16).astype(F32)


def split_pool(pool_ref, code_ref):
    cols = pool_ref.shape[2]
    pages, page = code_ref.shape
    i = lax.broadcasted_iota(I32, (2 * page, 2 * page), 0)
    j = lax.broadcasted_iota(I32, (2 * page, 2 * page), 1)
    pick = jnp.where(j == 2 * (i % page) + i // page, 1.0, 0.0).astype(BF16)
    keys, values = [], []
    for p in range(pages):
        both = pool_ref[p * page : (p + 1) * page].reshape(2 * page, cols)
        apart = jnp.dot(pick, both, preferred_element_type=F32)
        keys.append(apart[:page].astype(BF16))
        values.append(apart[page:].T.astype(BF16))
    return jnp.concatenate(keys, axis=0), jnp.concatenate(values, axis=1), slot_terms(code_ref)


def slot_terms(code_ref):
    pages, page = code_ref.shape
    sub = lax.broadcasted_iota(I32, (128, page), 0)
    blocks = []
    for p in range(pages):
        code = jnp.broadcast_to(code_ref[p : p + 1, :], (128, page))
        hit = ((code == sub % 8) & (sub < 24)) | ((sub >= 24) & (sub < 27))
        term = jnp.where(hit, 1.0, 0.0)
        term = jnp.where((sub == 27) & (code == 8), FAR, term)
        blocks.append(term.T.astype(BF16))
    return jnp.concatenate(blocks, axis=0)


def row_terms(bias, variate):
    rows = variate.shape[1]
    sub = lax.broadcasted_iota(I32, (8, rows), 0)
    hit = variate == sub
    other, step = split3(bias[1:2, :]), split3(bias[2:3, :])
    picked = [jnp.where(hit, jnp.broadcast_to(piece, (8, rows)), 0.0) for piece in step]
    tail = jnp.where(sub == 3, 1.0, 0.0)
    for at, piece in enumerate(other):
        tail = jnp.where(sub == at, piece, tail)
    top = jnp.concatenate(picked + [tail], axis=0).astype(BF16)
    return jnp.concatenate([top, jnp.zeros((96, rows), BF16)], axis=0)


def query_terms(q, rows_ref, variate):
    blocks = variate.shape[1] // rows_ref.shape[1]
    cats = []
    for head in range(q.shape[0] // HD):
        q_head = q[head * HD : (head + 1) * HD, :]
        zero = jnp.zeros_like(q_head)
        both = [q_head, zero] if head % 2 == 0 else [zero, q_head]
        cats.append(jnp.concatenate(both + [row_terms(wide(rows_ref, head, blocks), variate)], axis=0))
    return cats


def attend(cats, node):
    keys, values_t, terms = node
    scores = []
    for head, cat in enumerate(cats):
        pair = head // 2
        k_cat = jnp.concatenate([keys[:, pair * 128 : (pair + 1) * 128], terms], axis=1)
        scores.append(jnp.dot(k_cat, cat, preferred_element_type=F32))
    done = []
    for head, score in enumerate(scores):
        peak = jnp.max(score, axis=0, keepdims=True)
        weights = jnp.exp(score - peak)
        total = jnp.sum(weights, axis=0, keepdims=True)
        mixed = jnp.dot(values_t[head * HD : (head + 1) * HD, :], weights.astype(BF16), preferred_element_type=F32)
        done.append(((mixed / total).astype(BF16), peak + jnp.log(total)))
    return done


def wide(rows_ref, head, blocks):
    return jnp.concatenate([rows_ref[8 * head : 8 * head + 8, :]] * blocks, axis=1)


def gather_rows(msgs, cols):
    q = jnp.concatenate([msg[:cols, :] for msg in msgs], axis=1)
    aux = jnp.concatenate([msg[cols:, :].astype(F32).astype(I32) for msg in msgs], axis=1)
    return q, aux


def own_kernel(normed_ref, w_ref, pool_ref, code_ref, k_ref, v_ref, keys_ref, values_ref, terms_ref):
    for i, own_ref in ((1, k_ref), (2, v_ref)):
        own = jnp.dot(normed_ref[...], w_ref[i], preferred_element_type=F32).astype(BF16)
        own_ref[...] = own.astype(F32).T.astype(BF16)
    keys_ref[...], values_ref[...], terms_ref[...] = split_pool(pool_ref, code_ref)


def pair_terms(rows_ref, mine, theirs, msgs, outs):
    count = len(msgs)
    cols = mine[0].shape[1]
    rows = msgs[0].shape[1]
    q, aux = gather_rows(msgs, cols)
    cats = query_terms(q, rows_ref, aux[0:1, :])
    me = lax.axis_index("seq")
    mate = me ^ jnp.where(lax.axis_index("tp") % 2 == 0, MATES[0], MATES[1])
    named = lambda node: jnp.max((aux[1:4, :] == node).astype(I32), axis=0, keepdims=True) > 0
    named_1, named_2 = named(me), named(mate)
    pieces = []
    for head, ((o1, lse1), (o2, lse2)) in enumerate(zip(attend(cats, mine), attend(cats, theirs))):
        lse1 = jnp.where(named_1, lse1, FAR)
        lse2 = jnp.where(named_2, lse2, FAR)
        top = jnp.maximum(lse1, lse2)
        w1, w2 = jnp.exp(lse1 - top), jnp.exp(lse2 - top)
        merged = ((w1 * o1.astype(F32) + w2 * o2.astype(F32)) / (w1 + w2)).astype(BF16)
        for b, out in enumerate(outs):
            out[head * HD : (head + 1) * HD, :] = merged[:, b * rows : (b + 1) * rows]
        pieces += split3(top + jnp.log(w1 + w2))
    pieces.append(jnp.zeros((AUX - len(pieces), count * rows), F32))
    tail = jnp.concatenate(pieces, axis=0).astype(BF16)
    for b, out in enumerate(outs):
        out[cols:, :] = tail[:, b * rows : (b + 1) * rows]


def far_kernel(rows_ref, keys_ref, values_ref, terms_ref, pool_ref, code_ref, *refs):
    count = (len(refs) - 3) // 2
    mate = split_pool(pool_ref, code_ref)
    pair_terms(rows_ref, (keys_ref[...], values_ref[...], terms_ref[...]), mate, refs[:count], refs[count : 2 * count])
    for ref, value in zip(refs[2 * count :], mate):
        ref[...] = value


def near_kernel(rows_ref, *refs):
    nodes, refs = [ref[...] for ref in refs[:6]], refs[6:]
    count = len(refs) // 2
    pair_terms(rows_ref, nodes[:3], nodes[3:], refs[:count], refs[count:])


def add_parts(acc, parts, cols):
    auxes = [part[cols:, :].astype(F32) for part in parts]
    for head, (top, whole, total) in enumerate(acc):
        at = slice(head * HD, (head + 1) * HD)
        lses = [sum(aux[3 * head + i : 3 * head + i + 1, :] for i in range(3)) for aux in auxes]
        peak = top
        for lse in lses:
            peak = jnp.maximum(peak, lse)
        weight = jnp.exp(top - peak)
        whole, total = weight * whole, weight * total
        for lse, part in zip(lses, parts):
            weight = jnp.exp(lse - peak)
            whole = whole + weight
            total = total + weight * part[at, :].astype(F32)
        yield peak, whole, total


def combine_far_kernel(rows_ref, q_ref, k_ref, v_ref, *refs):
    *parts, acc_ref, side_ref = refs
    cols = k_ref.shape[0]
    acc = []
    for head in range(cols // HD):
        at = slice(head * HD, (head + 1) * HD)
        q, k = q_ref[at, :].astype(F32), k_ref[at, :].astype(F32)
        own = jnp.sum(q * k, axis=0, keepdims=True) + rows_ref[8 * head : 8 * head + 1, :]
        acc.append((own, jnp.ones_like(own), v_ref[at, :].astype(F32)))
    for head, (top, whole, total) in enumerate(add_parts(acc, parts, cols)):
        acc_ref[head * HD : (head + 1) * HD, :] = total
        side_ref[2 * head : 2 * head + 2, :] = jnp.concatenate([top, whole], axis=0)


def combine_near_kernel(acc_ref, side_ref, *refs):
    *parts, attn_ref = refs
    cols = acc_ref.shape[0]
    acc = [
        (side_ref[2 * head : 2 * head + 1, :], side_ref[2 * head + 1 : 2 * head + 2, :], acc_ref[head * HD : (head + 1) * HD, :])
        for head in range(cols // HD)
    ]
    done = [total / whole for _, whole, total in add_parts(acc, parts, cols)]
    attn_ref[...] = jnp.concatenate(done, axis=0).T.astype(BF16)


def project_kernel(base_ref, *refs):
    *pairs, out_ref = refs
    half = len(pairs) // 2
    total = base_ref[...].astype(F32)
    for attn, w in zip(pairs[:half], pairs[half:]):
        total = total + jnp.dot(attn[...], w[...], preferred_element_type=F32)
    out_ref[...] = total.astype(out_ref.dtype)


def last_kernel(base_ref, *refs):
    *pairs, out_hbm, out_ref, sems = refs
    half = len(pairs) // 2
    step = 256
    copies = []
    for i, at in enumerate(range(0, base_ref.shape[1], step)):
        span = slice(at, at + step)
        total = base_ref[:, span]
        for attn, w in zip(pairs[:half], pairs[half:]):
            total = total + jnp.dot(attn[...], w[:, span], preferred_element_type=F32)
        out_ref[:, span] = total.astype(out_ref.dtype)
        copies.append(pltpu.make_async_copy(out_ref.at[:, span], out_hbm.at[:, span], sems.at[i]))
        copies[-1].start()
    for copy in copies:
        copy.wait()


def swap(x, masks):
    owners, parts = lax.axis_size("seq"), lax.axis_size("tp")
    pairs = [(i * parts + t, (i ^ masks[t % 2]) * parts + t) for i in range(owners) for t in range(parts)]
    return lax.ppermute(x, ("seq", "tp"), pairs)


def across(x, mask):
    return lax.ppermute(x, "tp", [(t, t ^ mask) for t in range(lax.axis_size("tp"))])


def dense_body(
    tokens,
    norm_gain,
    w_qkv,
    w_out,
    head_bias,
    kv_pool,
    key_variate,
    page_table,
    node_len,
    path_nodes,
    query_variate,
):
    rows, width = tokens.shape
    cols = w_qkv.shape[2]
    heads = cols // HD
    pages, page = key_variate.shape
    slots = pages * page

    pool = kv_pool.reshape(slots, 2, cols)
    pool2 = swap(pool, MATES)

    w3 = w_qkv.transpose(1, 0, 2)
    msg, normed, bias, tok, pool, code = call(
        query_kernel,
        [
            shape(cols + AUX, rows), shape(rows, width), shape(8 * heads, rows, dtype=F32), shape(rows, width),
            shape(slots, 2, cols), shape(pages, page, dtype=I32),
        ],
        node_len, tokens, norm_gain[None], w3, query_variate[None], path_nodes.T, head_bias, key_variate, page_table,
        pool,
        away=range(1, 10),
        scratch=[
            pltpu.VMEM((1, width), F32), pltpu.VMEM((width, cols), BF16), pltpu.VMEM((1, rows), I32), pltpu.VMEM((3, rows), I32),
            pltpu.VMEM((2, heads), F32), pltpu.VMEM((pages, page), I32), pltpu.SMEM((1, pages), I32),
            pltpu.SemaphoreType.DMA((9,)),
        ],
    )
    msgs = [msg] + [swap(msg, peer) for peer in PEERS]
    code2 = swap(code, MATES)

    key, value, keys, values_t, terms = call(
        own_kernel,
        [
            shape(cols, rows), shape(cols, rows), shape(slots, cols), shape(cols, slots), shape(slots, 128),
        ],
        normed, w3, pool, code,
        flops=115300000,
    )
    w_far = across(w_out, 2)
    far = len(PEERS) - 1
    node = [shape(slots, cols), shape(cols, slots), shape(slots, 128)]
    message = shape(cols + AUX, rows)
    *far_out, keys2, values2, terms2 = call(
        far_kernel, [message] * far + node, bias, keys, values_t, terms, pool2, code2, *msgs[1 : 1 + far], flops=2306000000
    )
    own_out, near_out = call(
        near_kernel, [message] * 2, bias, keys, values_t, terms, keys2, values2, terms2, msgs[0], msgs[-1], flops=2306000000
    )
    far_back = [swap(m, peer) for m, peer in zip(far_out, PEERS)]
    near_back = swap(near_out, PEERS[-1])
    acc, side = call(
        combine_far_kernel, [shape(cols, rows, dtype=F32), shape(2 * heads, rows, dtype=F32)],
        bias, msg, key, value, own_out, *far_back,
        flops=4612000000,
    )
    w_own, w_far, acc = lax.optimization_barrier((w_out, w_far, acc))
    w_near, w_last = across(w_own, 1), across(w_far, 1)
    attn = call(combine_near_kernel, shape(rows, cols), acc, side, near_back, flops=4612000000)
    x_near, x_far, x_last = (across(attn, k) for k in (1, 2, 3))
    total = call(project_kernel, shape(rows, width, dtype=F32), tok, attn, x_near, w_own, w_near)
    return call(
        last_kernel, shape(rows, width), total, x_far, x_last, w_far, w_last,
        scratch=[pltpu.VMEM((rows, width), BF16), pltpu.SemaphoreType.DMA((width // 256,))],
        leaves=True,
    )


def solution(mesh):
    in_specs = (
        P("seq", None),
        P(),
        P(None, None, "tp"),
        P("tp", None),
        P(None, "tp"),
        P("seq", None, None, "tp"),
        P("seq", None),
        P("seq", None),
        P("seq"),
        P("seq", None),
        P("seq"),
    )
    out_specs = P("seq", None)
    owners, parts = mesh.shape["seq"], mesh.shape["tp"]
    dense = owners == 8 and parts == 4
    body = dense_body if dense else routed_body
    return jax.shard_map(body, mesh=mesh, in_specs=in_specs, out_specs=out_specs, check_vma=False)
```

```python
import jax
import jax.numpy as jnp
from jax import lax
from jax.experimental import pallas as pl
from jax.experimental.pallas import tpu as pltpu
from jax.sharding import PartitionSpec as P

HD = 64


def head_attend(qh, kh, vh, same, bias_same, bias_diff, valid):
    scores = jnp.dot(qh, kh.T, preferred_element_type=jnp.float32) * HD ** (-0.5)
    scores = scores + jnp.where(same, bias_same, bias_diff)
    scores = jnp.where(valid[None, :], scores, -1e30)
    peak = jnp.max(scores, axis=1)
    weights = jnp.exp(scores - peak[:, None])
    total = jnp.sum(weights, axis=1)
    mixed = (
        jnp.dot(weights.astype(jnp.bfloat16), vh, preferred_element_type=jnp.float32)
        / total[:, None]
    )
    mixed = lax.optimization_barrier(mixed.astype(jnp.bfloat16))
    return (mixed, peak, total)


def place_rows(dest, values, variates, owners, slots):
    onehot = (dest[:, None] == jnp.arange(owners, dtype=jnp.int32)[None, :]).astype(jnp.int32)
    before = jnp.cumsum(onehot, axis=0) - onehot
    slot = jnp.sum(before * onehot, axis=1)
    flat = dest * slots + slot
    width = values.shape[1]
    qbuf = (
        jnp.zeros((owners * slots, width), jnp.bfloat16)
        .at[flat]
        .set(values)
        .reshape(owners, slots, width)
    )
    vbuf = jnp.zeros((owners * slots,), jnp.int32).at[flat].set(variates).reshape(owners, slots)
    return (qbuf, vbuf, flat)


def routed_body(
    tokens,
    norm_gain,
    w_qkv,
    w_out,
    head_bias,
    kv_pool,
    key_variate,
    page_table,
    node_len,
    path_nodes,
    query_variate,
):
    tok_rows, width = tokens.shape
    heads_here = w_qkv.shape[2] // HD
    owners = lax.axis_size("seq")
    slots = min(tok_rows, 8 * tok_rows // owners)
    xf = tokens.astype(jnp.float32)
    normed = (xf * lax.rsqrt(jnp.mean(xf * xf, axis=1, keepdims=True) + 1e-05) * norm_gain).astype(
        jnp.bfloat16
    )
    qkv = jnp.dot(
        normed, w_qkv.reshape(width, 3 * heads_here * HD), preferred_element_type=jnp.float32
    ).astype(jnp.bfloat16)
    qkv = qkv.reshape(tok_rows, 3, heads_here, HD)
    query, key, value = (qkv[:, 0], qkv[:, 1], qkv[:, 2])
    order = page_table[0]
    node_slots = kv_pool.shape[0] * kv_pool.shape[1]
    pages = kv_pool[order].reshape(node_slots, 2, heads_here, HD)
    node_keys = jnp.moveaxis(pages[:, 0], 1, 0)
    node_values = jnp.moveaxis(pages[:, 1], 1, 0)
    key_var = key_variate[order].reshape(node_slots)
    valid = jnp.arange(node_slots, dtype=jnp.int32) < node_len[0]
    qflat = query.reshape(tok_rows, heads_here * HD)
    out_list, peak_list, total_list = ([], [], [])
    for level in range(3):
        qbuf, vbuf, flat = place_rows(path_nodes[:, level], qflat, query_variate, owners, slots)
        owner_qbuf = lax.all_to_all(qbuf, "seq", split_axis=0, concat_axis=0, tiled=True)
        owner_vbuf = lax.all_to_all(vbuf, "seq", split_axis=0, concat_axis=0, tiled=True)
        sources, count, cols = owner_qbuf.shape
        rows = sources * count
        heads_q = jnp.moveaxis(owner_qbuf.reshape(rows, heads_here, HD), 1, 0)
        same = owner_vbuf.reshape(rows)[:, None] == key_var[None, :]

        def per_head(xs):
            return head_attend(xs[0], xs[1], xs[2], same, xs[3], xs[4], valid)

        mixed, peak, total = lax.map(
            per_head, (heads_q, node_keys, node_values, head_bias[1], head_bias[0])
        )
        mixed = jnp.moveaxis(mixed, 0, 1).reshape(sources, count, cols)
        peak = peak.T.reshape(sources, count, heads_here)
        total = total.T.reshape(sources, count, heads_here)
        mixed_back = lax.all_to_all(mixed, "seq", split_axis=0, concat_axis=0, tiled=True)
        peak_back = lax.all_to_all(peak, "seq", split_axis=0, concat_axis=0, tiled=True)
        total_back = lax.all_to_all(total, "seq", split_axis=0, concat_axis=0, tiled=True)
        mixed = mixed_back
        peak = peak_back
        total = total_back
        out_list.append(mixed.reshape(owners * slots, -1)[flat].reshape(tok_rows, heads_here, HD))
        peak_list.append(peak.reshape(owners * slots, heads_here)[flat])
        total_list.append(total.reshape(owners * slots, heads_here)[flat])
    outs = jnp.stack(out_list, axis=1)
    peaks = jnp.stack(peak_list, axis=1)
    totals = jnp.stack(total_list, axis=1)
    own_peak = (
        jnp.sum(query.astype(jnp.float32) * key.astype(jnp.float32), axis=2) * HD ** (-0.5)
        + head_bias[1][None, :]
    )
    all_o = jnp.concatenate([value.astype(jnp.float32)[:, None], outs.astype(jnp.float32)], axis=1)
    all_m = jnp.concatenate([own_peak[:, None], peaks], axis=1)
    all_l = jnp.concatenate([jnp.ones((tok_rows, 1, heads_here), jnp.float32), totals], axis=1)
    top = jnp.max(all_m, axis=1, keepdims=True)
    scale = all_l * jnp.exp(all_m - top)
    attn = (jnp.sum(scale[..., None] * all_o, axis=1) / jnp.sum(scale, axis=1)[..., None]).astype(
        jnp.bfloat16
    )
    partial_sum = jnp.dot(
        attn.reshape(tok_rows, heads_here * HD), w_out, preferred_element_type=jnp.float32
    )
    total_sum = lax.psum(partial_sum, "tp")
    return (xf + total_sum).astype(jnp.bfloat16)


BF16, F32, I32 = jnp.bfloat16, jnp.float32, jnp.int32
AUX = 16
FAR = -1e30
MATES = (1, 2)
PEERS = ((4, 5), (6, 4), (2, 1))
VMEM = pl.BlockSpec(memory_space=pltpu.VMEM)
HBM = pl.BlockSpec(memory_space=pltpu.HBM)
SMEM = pl.BlockSpec(memory_space=pltpu.SMEM)


def call(kernel, outs, *args, flops=1, away=(), scratch=(), leaves=False):
    single = not isinstance(outs, (tuple, list))
    args = [pltpu.with_memory_space_constraint(a, pltpu.HBM) if i in away else a for i, a in enumerate(args)]
    return pl.pallas_call(
        kernel,
        out_shape=outs,
        scratch_shapes=scratch,
        in_specs=[HBM if i in away else SMEM if a.size == 1 else VMEM for i, a in enumerate(args)],
        out_specs=HBM if leaves else VMEM if single else [VMEM] * len(outs),
        compiler_params=pltpu.CompilerParams(vmem_limit_bytes=16 << 20),
        cost_estimate=pl.CostEstimate(flops=flops, bytes_accessed=1, transcendentals=0),
    )(*args)


def shape(*dims, dtype=BF16):
    return jax.ShapeDtypeStruct(dims, dtype)


def fetch(sems, *pairs):
    copies = [pltpu.make_async_copy(src, dst, sems.at[i]) for i, (src, dst) in enumerate(pairs)]
    for copy in copies:
        copy.start()
    return copies


def query_kernel(
    len_ref, tok_hbm, gain_hbm, w_hbm, variate_hbm, path_hbm, bias_hbm, slot_hbm, table_hbm,
    msg_ref, normed_ref, rows_ref, tok_ref, code_ref,
    gain_ref, w_ref, variate_ref, path_ref, bias_ref, slot_ref, table_ref, sems,
):
    pages, page = slot_ref.shape
    copies = fetch(
        sems, (tok_hbm, tok_ref), (w_hbm.at[0], w_ref), (gain_hbm, gain_ref), (variate_hbm, variate_ref), (path_hbm, path_ref),
        (bias_hbm, bias_ref), (slot_hbm, slot_ref), (table_hbm, table_ref),
    )
    for copy in copies[2:8]:
        copy.wait()
    rows, cols = tok_ref.shape[0], w_ref.shape[1]
    length = len_ref[0]
    offset = lax.broadcasted_iota(I32, (1, page), 1)
    for p in range(pages):
        place = sum(jnp.where(table_ref[0, i] == p, i, 0) for i in range(pages))
        code_ref[p : p + 1, :] = jnp.where(place * page + offset < length, slot_ref[p : p + 1, :], 8)
    for head in range(cols // HD):
        same = jnp.full((1, rows), bias_ref[1, head], F32)
        other = jnp.full((1, rows), bias_ref[0, head], F32)
        rows_ref[8 * head : 8 * head + 8, :] = jnp.concatenate([same, other, same - other, jnp.zeros((5, rows), F32)], axis=0)
    aux = [variate_ref[...].astype(F32), path_ref[...].astype(F32), jnp.zeros((AUX - 4, rows), F32)]
    msg_ref[cols:, :] = jnp.concatenate(aux, axis=0).astype(BF16)
    copies[0].wait()
    x = tok_ref[...].astype(F32)
    r = lax.rsqrt(jnp.mean(x * x, axis=1, keepdims=True) + 1e-05)
    normed = (x * r * gain_ref[...]).astype(BF16)
    normed_ref[...] = normed
    copies[1].wait()
    q = jnp.dot(normed, w_ref[...], preferred_element_type=F32).astype(BF16)
    msg_ref[:cols, :] = (q.astype(F32) * HD ** (-0.5)).T.astype(BF16)


def split3(x):
    a = x.astype(BF16).astype(F32)
    b = (x - a).astype(BF16).astype(F32)
    return a, b, (x - a - b).astype(BF16).astype(F32)


def split_pool(pool_ref, code_ref):
    cols = pool_ref.shape[2]
    pages, page = code_ref.shape
    i = lax.broadcasted_iota(I32, (2 * page, 2 * page), 0)
    j = lax.broadcasted_iota(I32, (2 * page, 2 * page), 1)
    pick = jnp.where(j == 2 * (i % page) + i // page, 1.0, 0.0).astype(BF16)
    keys, values = [], []
    for p in range(pages):
        both = pool_ref[p * page : (p + 1) * page].reshape(2 * page, cols)
        apart = jnp.dot(pick, both, preferred_element_type=F32)
        keys.append(apart[:page].astype(BF16))
        values.append(apart[page:].T.astype(BF16))
    return jnp.concatenate(keys, axis=0), jnp.concatenate(values, axis=1), slot_terms(code_ref)


def slot_terms(code_ref):
    pages, page = code_ref.shape
    sub = lax.broadcasted_iota(I32, (128, page), 0)
    blocks = []
    for p in range(pages):
        code = jnp.broadcast_to(code_ref[p : p + 1, :], (128, page))
        hit = ((code == sub % 8) & (sub < 24)) | ((sub >= 24) & (sub < 27))
        term = jnp.where(hit, 1.0, 0.0)
        term = jnp.where((sub == 27) & (code == 8), FAR, term)
        blocks.append(term.T.astype(BF16))
    return jnp.concatenate(blocks, axis=0)


def row_terms(bias, variate):
    rows = variate.shape[1]
    sub = lax.broadcasted_iota(I32, (8, rows), 0)
    hit = variate == sub
    other, step = split3(bias[1:2, :]), split3(bias[2:3, :])
    picked = [jnp.where(hit, jnp.broadcast_to(piece, (8, rows)), 0.0) for piece in step]
    tail = jnp.where(sub == 3, 1.0, 0.0)
    for at, piece in enumerate(other):
        tail = jnp.where(sub == at, piece, tail)
    top = jnp.concatenate(picked + [tail], axis=0).astype(BF16)
    return jnp.concatenate([top, jnp.zeros((96, rows), BF16)], axis=0)


def query_terms(q, rows_ref, variate):
    blocks = variate.shape[1] // rows_ref.shape[1]
    cats = []
    for head in range(q.shape[0] // HD):
        q_head = q[head * HD : (head + 1) * HD, :]
        zero = jnp.zeros_like(q_head)
        both = [q_head, zero] if head % 2 == 0 else [zero, q_head]
        cats.append(jnp.concatenate(both + [row_terms(wide(rows_ref, head, blocks), variate)], axis=0))
    return cats


def attend(cats, node):
    keys, values_t, terms = node
    scores = []
    for head, cat in enumerate(cats):
        pair = head // 2
        k_cat = jnp.concatenate([keys[:, pair * 128 : (pair + 1) * 128], terms], axis=1)
        scores.append(jnp.dot(k_cat, cat, preferred_element_type=F32))
    done = []
    for head, score in enumerate(scores):
        peak = jnp.max(score, axis=0, keepdims=True)
        weights = jnp.exp(score - peak)
        total = jnp.sum(weights, axis=0, keepdims=True)
        mixed = jnp.dot(values_t[head * HD : (head + 1) * HD, :], weights.astype(BF16), preferred_element_type=F32)
        done.append(((mixed / total).astype(BF16), peak + jnp.log(total)))
    return done


def wide(rows_ref, head, blocks):
    return jnp.concatenate([rows_ref[8 * head : 8 * head + 8, :]] * blocks, axis=1)


def gather_rows(msgs, cols):
    q = jnp.concatenate([msg[:cols, :] for msg in msgs], axis=1)
    aux = jnp.concatenate([msg[cols:, :].astype(F32).astype(I32) for msg in msgs], axis=1)
    return q, aux


def own_kernel(normed_ref, w_ref, pool_hbm, code_ref, k_ref, v_ref, keys_ref, values_ref, terms_ref, pool_ref, sem):
    copy = pltpu.make_async_copy(pool_hbm, pool_ref, sem)
    copy.start()
    for i, own_ref in ((1, k_ref), (2, v_ref)):
        own = jnp.dot(normed_ref[...], w_ref[i], preferred_element_type=F32).astype(BF16)
        own_ref[...] = own.astype(F32).T.astype(BF16)
    copy.wait()
    keys_ref[...], values_ref[...], terms_ref[...] = split_pool(pool_ref, code_ref)


def pair_terms(rows_ref, mine, theirs, msgs, outs):
    count = len(msgs)
    cols = mine[0].shape[1]
    rows = msgs[0].shape[1]
    q, aux = gather_rows(msgs, cols)
    cats = query_terms(q, rows_ref, aux[0:1, :])
    me = lax.axis_index("seq")
    mate = me ^ jnp.where(lax.axis_index("tp") % 2 == 0, MATES[0], MATES[1])
    named = lambda node: jnp.max((aux[1:4, :] == node).astype(I32), axis=0, keepdims=True) > 0
    named_1, named_2 = named(me), named(mate)
    pieces = []
    for head, ((o1, lse1), (o2, lse2)) in enumerate(zip(attend(cats, mine), attend(cats, theirs))):
        lse1 = jnp.where(named_1, lse1, FAR)
        lse2 = jnp.where(named_2, lse2, FAR)
        top = jnp.maximum(lse1, lse2)
        w1, w2 = jnp.exp(lse1 - top), jnp.exp(lse2 - top)
        merged = ((w1 * o1.astype(F32) + w2 * o2.astype(F32)) / (w1 + w2)).astype(BF16)
        for b, out in enumerate(outs):
            out[head * HD : (head + 1) * HD, :] = merged[:, b * rows : (b + 1) * rows]
        pieces += split3(top + jnp.log(w1 + w2))
    pieces.append(jnp.zeros((AUX - len(pieces), count * rows), F32))
    tail = jnp.concatenate(pieces, axis=0).astype(BF16)
    for b, out in enumerate(outs):
        out[cols:, :] = tail[:, b * rows : (b + 1) * rows]


def far_kernel(rows_ref, keys_ref, values_ref, terms_ref, pool_ref, code_ref, *refs):
    count = (len(refs) - 3) // 2
    mate = split_pool(pool_ref, code_ref)
    pair_terms(rows_ref, (keys_ref[...], values_ref[...], terms_ref[...]), mate, refs[:count], refs[count : 2 * count])
    for ref, value in zip(refs[2 * count :], mate):
        ref[...] = value


def near_kernel(rows_ref, *refs):
    nodes, refs = [ref[...] for ref in refs[:6]], refs[6:]
    count = len(refs) // 2
    pair_terms(rows_ref, nodes[:3], nodes[3:], refs[:count], refs[count:])


def add_parts(acc, parts, cols):
    auxes = [part[cols:, :].astype(F32) for part in parts]
    for head, (top, whole, total) in enumerate(acc):
        at = slice(head * HD, (head + 1) * HD)
        lses = [sum(aux[3 * head + i : 3 * head + i + 1, :] for i in range(3)) for aux in auxes]
        peak = top
        for lse in lses:
            peak = jnp.maximum(peak, lse)
        weight = jnp.exp(top - peak)
        whole, total = weight * whole, weight * total
        for lse, part in zip(lses, parts):
            weight = jnp.exp(lse - peak)
            whole = whole + weight
            total = total + weight * part[at, :].astype(F32)
        yield peak, whole, total


def combine_far_kernel(rows_ref, q_ref, k_ref, v_ref, *refs):
    *parts, acc_ref, side_ref = refs
    cols = k_ref.shape[0]
    acc = []
    for head in range(cols // HD):
        at = slice(head * HD, (head + 1) * HD)
        q, k = q_ref[at, :].astype(F32), k_ref[at, :].astype(F32)
        own = jnp.sum(q * k, axis=0, keepdims=True) + rows_ref[8 * head : 8 * head + 1, :]
        acc.append((own, jnp.ones_like(own), v_ref[at, :].astype(F32)))
    for head, (top, whole, total) in enumerate(add_parts(acc, parts, cols)):
        acc_ref[head * HD : (head + 1) * HD, :] = total
        side_ref[2 * head : 2 * head + 2, :] = jnp.concatenate([top, whole], axis=0)


def combine_near_kernel(acc_ref, side_ref, *refs):
    *parts, attn_ref = refs
    cols = acc_ref.shape[0]
    acc = [
        (side_ref[2 * head : 2 * head + 1, :], side_ref[2 * head + 1 : 2 * head + 2, :], acc_ref[head * HD : (head + 1) * HD, :])
        for head in range(cols // HD)
    ]
    done = [total / whole for _, whole, total in add_parts(acc, parts, cols)]
    attn_ref[...] = jnp.concatenate(done, axis=0).T.astype(BF16)


def project_kernel(base_ref, *refs):
    *pairs, out_ref = refs
    half = len(pairs) // 2
    total = base_ref[...].astype(F32)
    for attn, w in zip(pairs[:half], pairs[half:]):
        total = total + jnp.dot(attn[...], w[...], preferred_element_type=F32)
    out_ref[...] = total.astype(out_ref.dtype)


def last_kernel(base_ref, *refs):
    *pairs, out_hbm, out_ref, sems = refs
    half = len(pairs) // 2
    step = 256
    copies = []
    for i, at in enumerate(range(0, base_ref.shape[1], step)):
        span = slice(at, at + step)
        total = base_ref[:, span]
        for attn, w in zip(pairs[:half], pairs[half:]):
            total = total + jnp.dot(attn[...], w[:, span], preferred_element_type=F32)
        out_ref[:, span] = total.astype(out_ref.dtype)
        copies.append(pltpu.make_async_copy(out_ref.at[:, span], out_hbm.at[:, span], sems.at[i]))
        copies[-1].start()
    for copy in copies:
        copy.wait()


def swap(x, masks):
    owners, parts = lax.axis_size("seq"), lax.axis_size("tp")
    pairs = [(i * parts + t, (i ^ masks[t % 2]) * parts + t) for i in range(owners) for t in range(parts)]
    return lax.ppermute(x, ("seq", "tp"), pairs)


def across(x, mask):
    return lax.ppermute(x, "tp", [(t, t ^ mask) for t in range(lax.axis_size("tp"))])


def dense_body(
    tokens,
    norm_gain,
    w_qkv,
    w_out,
    head_bias,
    kv_pool,
    key_variate,
    page_table,
    node_len,
    path_nodes,
    query_variate,
):
    rows, width = tokens.shape
    cols = w_qkv.shape[2]
    heads = cols // HD
    pages, page = key_variate.shape
    slots = pages * page

    pool = kv_pool.reshape(slots, 2, cols)
    pool2 = swap(pool, MATES)

    w3 = w_qkv.transpose(1, 0, 2)
    msg, normed, bias, tok, code = call(
        query_kernel,
        [
            shape(cols + AUX, rows), shape(rows, width), shape(8 * heads, rows, dtype=F32), shape(rows, width),
            shape(pages, page, dtype=I32),
        ],
        node_len, tokens, norm_gain[None], w3, query_variate[None], path_nodes.T, head_bias, key_variate, page_table,
        away=range(1, 9),
        scratch=[
            pltpu.VMEM((1, width), F32), pltpu.VMEM((width, cols), BF16), pltpu.VMEM((1, rows), I32), pltpu.VMEM((3, rows), I32),
            pltpu.VMEM((2, heads), F32), pltpu.VMEM((pages, page), I32), pltpu.SMEM((1, pages), I32),
            pltpu.SemaphoreType.DMA((8,)),
        ],
    )
    msgs = [msg] + [swap(msg, peer) for peer in PEERS]
    code2 = swap(code, MATES)

    key, value, keys, values_t, terms = call(
        own_kernel,
        [
            shape(cols, rows), shape(cols, rows), shape(slots, cols), shape(cols, slots), shape(slots, 128),
        ],
        normed, w3, pool, code,
        flops=115300000,
        away=(2,),
        scratch=[pltpu.VMEM((slots, 2, cols), BF16), pltpu.SemaphoreType.DMA],
    )
    w_far = across(w_out, 2)
    far = len(PEERS) - 1
    node = [shape(slots, cols), shape(cols, slots), shape(slots, 128)]
    message = shape(cols + AUX, rows)
    *far_out, keys2, values2, terms2 = call(
        far_kernel, [message] * far + node, bias, keys, values_t, terms, pool2, code2, *msgs[1 : 1 + far], flops=2306000000
    )
    own_out, near_out = call(
        near_kernel, [message] * 2, bias, keys, values_t, terms, keys2, values2, terms2, msgs[0], msgs[-1], flops=2306000000
    )
    far_back = [swap(m, peer) for m, peer in zip(far_out, PEERS)]
    near_back = swap(near_out, PEERS[-1])
    acc, side = call(
        combine_far_kernel, [shape(cols, rows, dtype=F32), shape(2 * heads, rows, dtype=F32)],
        bias, msg, key, value, own_out, *far_back,
        flops=4612000000,
    )
    w_own, w_far, acc = lax.optimization_barrier((w_out, w_far, acc))
    w_near, w_last = across(w_own, 1), across(w_far, 1)
    attn = call(combine_near_kernel, shape(rows, cols), acc, side, near_back, flops=4612000000)
    x_near, x_far, x_last = (across(attn, k) for k in (1, 2, 3))
    total = call(project_kernel, shape(rows, width, dtype=F32), tok, attn, x_near, w_own, w_near)
    return call(
        last_kernel, shape(rows, width), total, x_far, x_last, w_far, w_last,
        scratch=[pltpu.VMEM((rows, width), BF16), pltpu.SemaphoreType.DMA((width // 256,))],
        leaves=True,
    )


def solution(mesh):
    in_specs = (
        P("seq", None),
        P(),
        P(None, None, "tp"),
        P("tp", None),
        P(None, "tp"),
        P("seq", None, None, "tp"),
        P("seq", None),
        P("seq", None),
        P("seq"),
        P("seq", None),
        P("seq"),
    )
    out_specs = P("seq", None)
    owners, parts = mesh.shape["seq"], mesh.shape["tp"]
    dense = owners == 8 and parts == 4
    body = dense_body if dense else routed_body
    return jax.shard_map(body, mesh=mesh, in_specs=in_specs, out_specs=out_specs, check_vma=False)
```

```python
import jax
import jax.numpy as jnp
from jax import lax
from jax.experimental import pallas as pl
from jax.experimental.pallas import tpu as pltpu
from jax.sharding import PartitionSpec as P

HD = 64


def head_attend(qh, kh, vh, same, bias_same, bias_diff, valid):
    scores = jnp.dot(qh, kh.T, preferred_element_type=jnp.float32) * HD ** (-0.5)
    scores = scores + jnp.where(same, bias_same, bias_diff)
    scores = jnp.where(valid[None, :], scores, -1e30)
    peak = jnp.max(scores, axis=1)
    weights = jnp.exp(scores - peak[:, None])
    total = jnp.sum(weights, axis=1)
    mixed = (
        jnp.dot(weights.astype(jnp.bfloat16), vh, preferred_element_type=jnp.float32)
        / total[:, None]
    )
    mixed = lax.optimization_barrier(mixed.astype(jnp.bfloat16))
    return (mixed, peak, total)


def place_rows(dest, values, variates, owners, slots):
    onehot = (dest[:, None] == jnp.arange(owners, dtype=jnp.int32)[None, :]).astype(jnp.int32)
    before = jnp.cumsum(onehot, axis=0) - onehot
    slot = jnp.sum(before * onehot, axis=1)
    flat = dest * slots + slot
    width = values.shape[1]
    qbuf = (
        jnp.zeros((owners * slots, width), jnp.bfloat16)
        .at[flat]
        .set(values)
        .reshape(owners, slots, width)
    )
    vbuf = jnp.zeros((owners * slots,), jnp.int32).at[flat].set(variates).reshape(owners, slots)
    return (qbuf, vbuf, flat)


def routed_body(
    tokens,
    norm_gain,
    w_qkv,
    w_out,
    head_bias,
    kv_pool,
    key_variate,
    page_table,
    node_len,
    path_nodes,
    query_variate,
):
    tok_rows, width = tokens.shape
    heads_here = w_qkv.shape[2] // HD
    owners = lax.axis_size("seq")
    slots = min(tok_rows, 8 * tok_rows // owners)
    xf = tokens.astype(jnp.float32)
    normed = (xf * lax.rsqrt(jnp.mean(xf * xf, axis=1, keepdims=True) + 1e-05) * norm_gain).astype(
        jnp.bfloat16
    )
    qkv = jnp.dot(
        normed, w_qkv.reshape(width, 3 * heads_here * HD), preferred_element_type=jnp.float32
    ).astype(jnp.bfloat16)
    qkv = qkv.reshape(tok_rows, 3, heads_here, HD)
    query, key, value = (qkv[:, 0], qkv[:, 1], qkv[:, 2])
    order = page_table[0]
    node_slots = kv_pool.shape[0] * kv_pool.shape[1]
    pages = kv_pool[order].reshape(node_slots, 2, heads_here, HD)
    node_keys = jnp.moveaxis(pages[:, 0], 1, 0)
    node_values = jnp.moveaxis(pages[:, 1], 1, 0)
    key_var = key_variate[order].reshape(node_slots)
    valid = jnp.arange(node_slots, dtype=jnp.int32) < node_len[0]
    qflat = query.reshape(tok_rows, heads_here * HD)
    out_list, peak_list, total_list = ([], [], [])
    for level in range(3):
        qbuf, vbuf, flat = place_rows(path_nodes[:, level], qflat, query_variate, owners, slots)
        owner_qbuf = lax.all_to_all(qbuf, "seq", split_axis=0, concat_axis=0, tiled=True)
        owner_vbuf = lax.all_to_all(vbuf, "seq", split_axis=0, concat_axis=0, tiled=True)
        sources, count, cols = owner_qbuf.shape
        rows = sources * count
        heads_q = jnp.moveaxis(owner_qbuf.reshape(rows, heads_here, HD), 1, 0)
        same = owner_vbuf.reshape(rows)[:, None] == key_var[None, :]

        def per_head(xs):
            return head_attend(xs[0], xs[1], xs[2], same, xs[3], xs[4], valid)

        mixed, peak, total = lax.map(
            per_head, (heads_q, node_keys, node_values, head_bias[1], head_bias[0])
        )
        mixed = jnp.moveaxis(mixed, 0, 1).reshape(sources, count, cols)
        peak = peak.T.reshape(sources, count, heads_here)
        total = total.T.reshape(sources, count, heads_here)
        mixed_back = lax.all_to_all(mixed, "seq", split_axis=0, concat_axis=0, tiled=True)
        peak_back = lax.all_to_all(peak, "seq", split_axis=0, concat_axis=0, tiled=True)
        total_back = lax.all_to_all(total, "seq", split_axis=0, concat_axis=0, tiled=True)
        mixed = mixed_back
        peak = peak_back
        total = total_back
        out_list.append(mixed.reshape(owners * slots, -1)[flat].reshape(tok_rows, heads_here, HD))
        peak_list.append(peak.reshape(owners * slots, heads_here)[flat])
        total_list.append(total.reshape(owners * slots, heads_here)[flat])
    outs = jnp.stack(out_list, axis=1)
    peaks = jnp.stack(peak_list, axis=1)
    totals = jnp.stack(total_list, axis=1)
    own_peak = (
        jnp.sum(query.astype(jnp.float32) * key.astype(jnp.float32), axis=2) * HD ** (-0.5)
        + head_bias[1][None, :]
    )
    all_o = jnp.concatenate([value.astype(jnp.float32)[:, None], outs.astype(jnp.float32)], axis=1)
    all_m = jnp.concatenate([own_peak[:, None], peaks], axis=1)
    all_l = jnp.concatenate([jnp.ones((tok_rows, 1, heads_here), jnp.float32), totals], axis=1)
    top = jnp.max(all_m, axis=1, keepdims=True)
    scale = all_l * jnp.exp(all_m - top)
    attn = (jnp.sum(scale[..., None] * all_o, axis=1) / jnp.sum(scale, axis=1)[..., None]).astype(
        jnp.bfloat16
    )
    partial_sum = jnp.dot(
        attn.reshape(tok_rows, heads_here * HD), w_out, preferred_element_type=jnp.float32
    )
    total_sum = lax.psum(partial_sum, "tp")
    return (xf + total_sum).astype(jnp.bfloat16)


BF16, F32, I32 = jnp.bfloat16, jnp.float32, jnp.int32
AUX = 16
FAR = -1e30
MATES = (1, 2)
PEERS = ((4, 5), (6, 4), (2, 1))
VMEM = pl.BlockSpec(memory_space=pltpu.VMEM)
HBM = pl.BlockSpec(memory_space=pltpu.HBM)
SMEM = pl.BlockSpec(memory_space=pltpu.SMEM)


def call(kernel, outs, *args, flops=1, away=(), scratch=(), leaves=False):
    single = not isinstance(outs, (tuple, list))
    args = [pltpu.with_memory_space_constraint(a, pltpu.HBM) if i in away else a for i, a in enumerate(args)]
    return pl.pallas_call(
        kernel,
        out_shape=outs,
        scratch_shapes=scratch,
        in_specs=[HBM if i in away else SMEM if a.size == 1 else VMEM for i, a in enumerate(args)],
        out_specs=HBM if leaves else VMEM if single else [VMEM] * len(outs),
        compiler_params=pltpu.CompilerParams(vmem_limit_bytes=16 << 20),
        cost_estimate=pl.CostEstimate(flops=flops, bytes_accessed=1, transcendentals=0),
    )(*args)


def shape(*dims, dtype=BF16):
    return jax.ShapeDtypeStruct(dims, dtype)


def fetch(sems, *pairs):
    copies = [pltpu.make_async_copy(src, dst, sems.at[i]) for i, (src, dst) in enumerate(pairs)]
    for copy in copies:
        copy.start()
    return copies


def query_kernel(
    len_ref, tok_hbm, gain_hbm, w_hbm, variate_hbm, path_hbm, bias_hbm, slot_hbm, table_hbm, pool_hbm,
    msg_ref, normed_ref, rows_ref, tok_ref, pool_ref, code_ref,
    gain_ref, w_ref, variate_ref, path_ref, bias_ref, slot_ref, table_ref, sems,
):
    pages, page = slot_ref.shape
    copies = fetch(
        sems, (tok_hbm, tok_ref), (w_hbm.at[0], w_ref), (gain_hbm, gain_ref), (variate_hbm, variate_ref), (path_hbm, path_ref),
        (bias_hbm, bias_ref), (slot_hbm, slot_ref), (table_hbm, table_ref), (pool_hbm, pool_ref),
    )
    for copy in copies[2:8]:
        copy.wait()
    rows, cols = tok_ref.shape[0], w_ref.shape[1]
    length = len_ref[0]
    offset = lax.broadcasted_iota(I32, (1, page), 1)
    for p in range(pages):
        place = sum(jnp.where(table_ref[0, i] == p, i, 0) for i in range(pages))
        code_ref[p : p + 1, :] = jnp.where(place * page + offset < length, slot_ref[p : p + 1, :], 8)
    for head in range(cols // HD):
        same = jnp.full((1, rows), bias_ref[1, head], F32)
        other = jnp.full((1, rows), bias_ref[0, head], F32)
        rows_ref[8 * head : 8 * head + 8, :] = jnp.concatenate([same, other, same - other, jnp.zeros((5, rows), F32)], axis=0)
    aux = [variate_ref[...].astype(F32), path_ref[...].astype(F32), jnp.zeros((AUX - 4, rows), F32)]
    msg_ref[cols:, :] = jnp.concatenate(aux, axis=0).astype(BF16)
    copies[0].wait()
    x = tok_ref[...].astype(F32)
    r = lax.rsqrt(jnp.mean(x * x, axis=1, keepdims=True) + 1e-05)
    normed = (x * r * gain_ref[...]).astype(BF16)
    normed_ref[...] = normed
    copies[1].wait()
    q = jnp.dot(normed, w_ref[...], preferred_element_type=F32).astype(BF16)
    msg_ref[:cols, :] = (q.astype(F32) * HD ** (-0.5)).T.astype(BF16)
    copies[8].wait()


def split3(x):
    a = x.astype(BF16).astype(F32)
    b = (x - a).astype(BF16).astype(F32)
    return a, b, (x - a - b).astype(BF16).astype(F32)


def split_pool(pool_ref, code_ref):
    cols = pool_ref.shape[2]
    pages, page = code_ref.shape
    i = lax.broadcasted_iota(I32, (2 * page, 2 * page), 0)
    j = lax.broadcasted_iota(I32, (2 * page, 2 * page), 1)
    pick = jnp.where(j == 2 * (i % page) + i // page, 1.0, 0.0).astype(BF16)
    keys, values = [], []
    for p in range(pages):
        both = pool_ref[p * page : (p + 1) * page].reshape(2 * page, cols)
        apart = jnp.dot(pick, both, preferred_element_type=F32)
        keys.append(apart[:page].astype(BF16))
        values.append(apart[page:].T.astype(BF16))
    return jnp.concatenate(keys, axis=0), jnp.concatenate(values, axis=1), slot_terms(code_ref)


def slot_terms(code_ref):
    pages, page = code_ref.shape
    sub = lax.broadcasted_iota(I32, (128, page), 0)
    blocks = []
    for p in range(pages):
        code = jnp.broadcast_to(code_ref[p : p + 1, :], (128, page))
        hit = ((code == sub % 8) & (sub < 24)) | ((sub >= 24) & (sub < 27))
        term = jnp.where(hit, 1.0, 0.0)
        term = jnp.where((sub == 27) & (code == 8), FAR, term)
        blocks.append(term.T.astype(BF16))
    return jnp.concatenate(blocks, axis=0)


def row_terms(bias, variate):
    rows = variate.shape[1]
    sub = lax.broadcasted_iota(I32, (8, rows), 0)
    hit = variate == sub
    other, step = split3(bias[1:2, :]), split3(bias[2:3, :])
    picked = [jnp.where(hit, jnp.broadcast_to(piece, (8, rows)), 0.0) for piece in step]
    tail = jnp.where(sub == 3, 1.0, 0.0)
    for at, piece in enumerate(other):
        tail = jnp.where(sub == at, piece, tail)
    top = jnp.concatenate(picked + [tail], axis=0).astype(BF16)
    return jnp.concatenate([top, jnp.zeros((96, rows), BF16)], axis=0)


def query_terms(q, rows_ref, variate):
    blocks = variate.shape[1] // rows_ref.shape[1]
    cats = []
    for head in range(q.shape[0] // HD):
        q_head = q[head * HD : (head + 1) * HD, :]
        zero = jnp.zeros_like(q_head)
        both = [q_head, zero] if head % 2 == 0 else [zero, q_head]
        cats.append(jnp.concatenate(both + [row_terms(wide(rows_ref, head, blocks), variate)], axis=0))
    return cats


def attend(cats, node):
    keys, values_t, terms = node
    scores = []
    for head, cat in enumerate(cats):
        pair = head // 2
        k_cat = jnp.concatenate([keys[:, pair * 128 : (pair + 1) * 128], terms], axis=1)
        scores.append(jnp.dot(k_cat, cat, preferred_element_type=F32))
    done = []
    for head, score in enumerate(scores):
        peak = jnp.max(score, axis=0, keepdims=True)
        weights = jnp.exp(score - peak)
        total = jnp.sum(weights, axis=0, keepdims=True)
        mixed = jnp.dot(values_t[head * HD : (head + 1) * HD, :], weights.astype(BF16), preferred_element_type=F32)
        done.append(((mixed / total).astype(BF16), peak + jnp.log(total)))
    return done


def wide(rows_ref, head, blocks):
    return jnp.concatenate([rows_ref[8 * head : 8 * head + 8, :]] * blocks, axis=1)


def gather_rows(msgs, cols):
    q = jnp.concatenate([msg[:cols, :] for msg in msgs], axis=1)
    aux = jnp.concatenate([msg[cols:, :].astype(F32).astype(I32) for msg in msgs], axis=1)
    return q, aux


def own_kernel(normed_ref, w_ref, pool_ref, code_ref, k_ref, v_ref, keys_ref, values_ref, terms_ref):
    for i, own_ref in ((1, k_ref), (2, v_ref)):
        own = jnp.dot(normed_ref[...], w_ref[i], preferred_element_type=F32).astype(BF16)
        own_ref[...] = own.astype(F32).T.astype(BF16)
    keys_ref[...], values_ref[...], terms_ref[...] = split_pool(pool_ref, code_ref)


def pair_terms(rows_ref, mine, theirs, msgs, outs):
    count = len(msgs)
    cols = mine[0].shape[1]
    rows = msgs[0].shape[1]
    q, aux = gather_rows(msgs, cols)
    cats = query_terms(q, rows_ref, aux[0:1, :])
    me = lax.axis_index("seq")
    mate = me ^ jnp.where(lax.axis_index("tp") % 2 == 0, MATES[0], MATES[1])
    named = lambda node: jnp.max((aux[1:4, :] == node).astype(I32), axis=0, keepdims=True) > 0
    named_1, named_2 = named(me), named(mate)
    pieces = []
    for head, ((o1, lse1), (o2, lse2)) in enumerate(zip(attend(cats, mine), attend(cats, theirs))):
        lse1 = jnp.where(named_1, lse1, FAR)
        lse2 = jnp.where(named_2, lse2, FAR)
        top = jnp.maximum(lse1, lse2)
        w1, w2 = jnp.exp(lse1 - top), jnp.exp(lse2 - top)
        merged = ((w1 * o1.astype(F32) + w2 * o2.astype(F32)) / (w1 + w2)).astype(BF16)
        for b, out in enumerate(outs):
            out[head * HD : (head + 1) * HD, :] = merged[:, b * rows : (b + 1) * rows]
        pieces += split3(top + jnp.log(w1 + w2))
    pieces.append(jnp.zeros((AUX - len(pieces), count * rows), F32))
    tail = jnp.concatenate(pieces, axis=0).astype(BF16)
    for b, out in enumerate(outs):
        out[cols:, :] = tail[:, b * rows : (b + 1) * rows]


def far_kernel(rows_ref, keys_ref, values_ref, terms_ref, pool_ref, code_ref, *refs):
    count = (len(refs) - 3) // 2
    mate = split_pool(pool_ref, code_ref)
    pair_terms(rows_ref, (keys_ref[...], values_ref[...], terms_ref[...]), mate, refs[:count], refs[count : 2 * count])
    for ref, value in zip(refs[2 * count :], mate):
        ref[...] = value


def near_kernel(rows_ref, *refs):
    nodes, refs = [ref[...] for ref in refs[:6]], refs[6:]
    count = len(refs) // 2
    pair_terms(rows_ref, nodes[:3], nodes[3:], refs[:count], refs[count:])


def add_parts(acc, parts, cols):
    auxes = [part[cols:, :].astype(F32) for part in parts]
    for head, (top, whole, total) in enumerate(acc):
        at = slice(head * HD, (head + 1) * HD)
        lses = [sum(aux[3 * head + i : 3 * head + i + 1, :] for i in range(3)) for aux in auxes]
        peak = top
        for lse in lses:
            peak = jnp.maximum(peak, lse)
        weight = jnp.exp(top - peak)
        whole, total = weight * whole, weight * total
        for lse, part in zip(lses, parts):
            weight = jnp.exp(lse - peak)
            whole = whole + weight
            total = total + weight * part[at, :].astype(F32)
        yield peak, whole, total


def combine_far_kernel(rows_ref, q_ref, k_ref, v_ref, *refs):
    *parts, acc_ref, side_ref = refs
    cols = k_ref.shape[0]
    acc = []
    for head in range(cols // HD):
        at = slice(head * HD, (head + 1) * HD)
        q, k = q_ref[at, :].astype(F32), k_ref[at, :].astype(F32)
        own = jnp.sum(q * k, axis=0, keepdims=True) + rows_ref[8 * head : 8 * head + 1, :]
        acc.append((own, jnp.ones_like(own), v_ref[at, :].astype(F32)))
    for head, (top, whole, total) in enumerate(add_parts(acc, parts, cols)):
        acc_ref[head * HD : (head + 1) * HD, :] = total
        side_ref[2 * head : 2 * head + 2, :] = jnp.concatenate([top, whole], axis=0)


def combine_near_kernel(acc_ref, side_ref, *refs):
    *parts, attn_ref = refs
    cols = acc_ref.shape[0]
    acc = [
        (side_ref[2 * head : 2 * head + 1, :], side_ref[2 * head + 1 : 2 * head + 2, :], acc_ref[head * HD : (head + 1) * HD, :])
        for head in range(cols // HD)
    ]
    done = [total / whole for _, whole, total in add_parts(acc, parts, cols)]
    attn_ref[...] = jnp.concatenate(done, axis=0).T.astype(BF16)


def project_kernel(base_ref, *refs):
    *pairs, out_ref = refs
    half = len(pairs) // 2
    total = base_ref[...].astype(F32)
    for attn, w in zip(pairs[:half], pairs[half:]):
        total = total + jnp.dot(attn[...], w[...], preferred_element_type=F32)
    out_ref[...] = total.astype(out_ref.dtype)


def last_kernel(base_ref, *refs):
    *pairs, out_hbm, out_ref, sems = refs
    half = len(pairs) // 2
    step = 512
    copies = []
    for i, at in enumerate(range(0, base_ref.shape[1], step)):
        span = slice(at, at + step)
        total = base_ref[:, span]
        for attn, w in zip(pairs[:half], pairs[half:]):
            total = total + jnp.dot(attn[...], w[:, span], preferred_element_type=F32)
        out_ref[:, span] = total.astype(out_ref.dtype)
        copies.append(pltpu.make_async_copy(out_ref.at[:, span], out_hbm.at[:, span], sems.at[i]))
        copies[-1].start()
    for copy in copies:
        copy.wait()


def swap(x, masks):
    owners, parts = lax.axis_size("seq"), lax.axis_size("tp")
    pairs = [(i * parts + t, (i ^ masks[t % 2]) * parts + t) for i in range(owners) for t in range(parts)]
    return lax.ppermute(x, ("seq", "tp"), pairs)


def across(x, mask):
    return lax.ppermute(x, "tp", [(t, t ^ mask) for t in range(lax.axis_size("tp"))])


def dense_body(
    tokens,
    norm_gain,
    w_qkv,
    w_out,
    head_bias,
    kv_pool,
    key_variate,
    page_table,
    node_len,
    path_nodes,
    query_variate,
):
    rows, width = tokens.shape
    cols = w_qkv.shape[2]
    heads = cols // HD
    pages, page = key_variate.shape
    slots = pages * page

    pool = kv_pool.reshape(slots, 2, cols)
    pool2 = swap(pool, MATES)

    w3 = w_qkv.transpose(1, 0, 2)
    msg, normed, bias, tok, pool, code = call(
        query_kernel,
        [
            shape(cols + AUX, rows), shape(rows, width), shape(8 * heads, rows, dtype=F32), shape(rows, width),
            shape(slots, 2, cols), shape(pages, page, dtype=I32),
        ],
        node_len, tokens, norm_gain[None], w3, query_variate[None], path_nodes.T, head_bias, key_variate, page_table,
        pool,
        away=range(1, 10),
        scratch=[
            pltpu.VMEM((1, width), F32), pltpu.VMEM((width, cols), BF16), pltpu.VMEM((1, rows), I32), pltpu.VMEM((3, rows), I32),
            pltpu.VMEM((2, heads), F32), pltpu.VMEM((pages, page), I32), pltpu.SMEM((1, pages), I32),
            pltpu.SemaphoreType.DMA((9,)),
        ],
    )
    msgs = [msg] + [swap(msg, peer) for peer in PEERS]
    code2 = swap(code, MATES)

    key, value, keys, values_t, terms = call(
        own_kernel,
        [
            shape(cols, rows), shape(cols, rows), shape(slots, cols), shape(cols, slots), shape(slots, 128),
        ],
        normed, w3, pool, code,
        flops=115300000,
    )
    w_far = across(w_out, 2)
    far = len(PEERS) - 1
    node = [shape(slots, cols), shape(cols, slots), shape(slots, 128)]
    message = shape(cols + AUX, rows)
    *far_out, keys2, values2, terms2 = call(
        far_kernel, [message] * far + node, bias, keys, values_t, terms, pool2, code2, *msgs[1 : 1 + far], flops=2306000000
    )
    own_out, near_out = call(
        near_kernel, [message] * 2, bias, keys, values_t, terms, keys2, values2, terms2, msgs[0], msgs[-1], flops=2306000000
    )
    far_back = [swap(m, peer) for m, peer in zip(far_out, PEERS)]
    near_back = swap(near_out, PEERS[-1])
    acc, side = call(
        combine_far_kernel, [shape(cols, rows, dtype=F32), shape(2 * heads, rows, dtype=F32)],
        bias, msg, key, value, own_out, *far_back,
        flops=4612000000,
    )
    w_own, w_far, acc = lax.optimization_barrier((w_out, w_far, acc))
    w_near, w_last = across(w_own, 1), across(w_far, 1)
    attn = call(combine_near_kernel, shape(rows, cols), acc, side, near_back, flops=4612000000)
    x_near, x_far, x_last = (across(attn, k) for k in (1, 2, 3))
    total = call(project_kernel, shape(rows, width, dtype=F32), tok, attn, x_near, w_own, w_near)
    return call(
        last_kernel, shape(rows, width), total, x_far, x_last, w_far, w_last,
        scratch=[pltpu.VMEM((rows, width), BF16), pltpu.SemaphoreType.DMA((width // 512,))],
        leaves=True,
    )


def solution(mesh):
    in_specs = (
        P("seq", None),
        P(),
        P(None, None, "tp"),
        P("tp", None),
        P(None, "tp"),
        P("seq", None, None, "tp"),
        P("seq", None),
        P("seq", None),
        P("seq"),
        P("seq", None),
        P("seq"),
    )
    out_specs = P("seq", None)
    owners, parts = mesh.shape["seq"], mesh.shape["tp"]
    dense = owners == 8 and parts == 4
    body = dense_body if dense else routed_body
    return jax.shard_map(body, mesh=mesh, in_specs=in_specs, out_specs=out_specs, check_vma=False)
```
